32 devices in a mesh: px: 2 (over y), py: 16 (over z, x, core).
Axes of the slice: x: 2, y: 2, z: 4, core: 2. Of those that a mesh axis runs over, the one named last changes fastest.
Arguments:
- velocity: float32 [3, 128, 128, 128], P(None, 'px', 'py'), may hold values from -4 to 4
- cotangent: float32 [3, 128, 128, 128], P(None, 'px', 'py'), may hold values from -6 to 6
- weight_in: bfloat16 [32, 3, 3, 3, 3], replicated, may hold values from -0.625 to 0.625
- bias_in: float32 [32], replicated, may hold values from -3 to 3
- weight_out: bfloat16 [6, 32, 3, 3, 3], replicated, may hold values from -0.21875 to 0.21875
Outputs:
- adjoint: float32 [3, 128, 128, 128], P(None, 'px', 'py')
The draws below stay inside these ranges and needn't reach their ends.
All inputs are finite; a program needn't handle non-finite values.
Results may differ from the reference program's by a relative error of at most 0.00041.
Values sent between devices are 32-bit elements; how exact they have to be, the bound alone decides.
A program may use at most 192 MiB of HBM per device.

```python
import math
import jax
import jax.numpy as jnp
from jax import lax

NX = 128
NY = 128
NZ = 128
HID = 32
COMP = 3
STRESS = 6
KS = 3


def block_levels(stream_key, dims, split, smallest, largest):
    factor_of = 1.0
    for axis_at, parts in split:
        steps = jax.random.uniform(jax.random.fold_in(jax.random.fold_in(stream_key, 6), axis_at), (parts,), jnp.float32, smallest / len(split), largest / len(split))
        factor_of = factor_of * jnp.repeat(jnp.exp(steps), dims[axis_at] // parts).reshape((-1,) + (1,) * (len(dims) - 1 - axis_at))
    return factor_of


def noise(own_key, shape, spread, reach, cuts=(), kind=jnp.bfloat16):
    values = spread * jax.random.normal(own_key, shape, jnp.float32)
    if cuts:
        values = values * block_levels(own_key, shape, cuts, -0.22, 0.18)
    return jnp.clip(values, -reach, reach).astype(kind)


def setup_inputs(seed: int = 0) -> dict:
    seeds = jax.random.split(jax.random.key(seed), 6)
    return {
        "velocity": noise(seeds[0], (COMP, NX, NY, NZ), 1.0, 4.0, ((1, 2), (2, 16)), jnp.float32),
        "cotangent": noise(seeds[1], (COMP, NX, NY, NZ), 1.0, 6.0, ((1, 2), (2, 16)), jnp.float32),
        "weight_in": noise(seeds[2], (HID, COMP, KS, KS, KS), (COMP * KS * KS * KS) ** -0.5, 0.625),
        "bias_in": noise(seeds[3], (HID,), 1.0, 3.0, (), jnp.float32),
        "weight_out": noise(seeds[4], (STRESS, HID, KS, KS, KS), (HID * KS * KS * KS) ** -0.5, 0.21875),
    }


time_step = 0.005


def shifted(source, spatial, offset, margin):
    slicers = [slice(None)]
    for position in range(1, 4):
        extent = source.shape[position]
        offset_now = offset if position == spatial else 0
        slicers.append(slice(margin + offset_now, extent - margin + offset_now))
    return source[tuple(slicers)]


def central(source, spatial, spacing):
    return (shifted(source, spatial, 1, 1) - shifted(source, spatial, -1, 1)) / (2.0 * spacing)


def sixth_order(source, spatial, spacing):
    first = shifted(source, spatial, 1, 3) - shifted(source, spatial, -1, 3)
    second = shifted(source, spatial, 2, 3) - shifted(source, spatial, -2, 3)
    third = shifted(source, spatial, 3, 3) - shifted(source, spatial, -3, 3)
    return (45.0 * first - 9.0 * second + third) / (60.0 * spacing)


def correlate(source, kernel):
    result = lax.conv_general_dilated(source[None], kernel, (1, 1, 1), "VALID",
                                      dimension_numbers=("NCDHW", "OIDHW", "NCDHW"),
                                      preferred_element_type=jnp.float32)
    return result[0]


def step_adjoint(vel_ext, lam_ext, weight_in, bias_in, weight_out, spacings):
    low_velocity = vel_ext[:, 1:-1, 1:-1, 1:-1].astype(jnp.bfloat16)
    pre_act = correlate(low_velocity, weight_in) + bias_in[:, None, None, None]
    tanh_slope = 1.0 - jnp.square(jnp.tanh(pre_act))
    lam_grads = [[central(lam_ext[component:component + 1], direction + 1, spacings[direction])[0]
                  for direction in range(3)] for component in range(3)]
    stress_adj = jnp.stack([lam_grads[0][0], lam_grads[1][1], lam_grads[2][2],
                            lam_grads[0][1] + lam_grads[1][0],
                            lam_grads[0][2] + lam_grads[2][0],
                            lam_grads[1][2] + lam_grads[2][1]]).astype(jnp.bfloat16)
    kernel_out = jnp.flip(weight_out, (2, 3, 4)).transpose(1, 0, 2, 3, 4)
    hidden_adj = correlate(stress_adj, kernel_out)
    pre_adj = (hidden_adj * tanh_slope).astype(jnp.bfloat16)
    kernel_in = jnp.flip(weight_in, (2, 3, 4)).transpose(1, 0, 2, 3, 4)
    closure_adj = correlate(pre_adj, kernel_in)
    lam_block = lam_ext[:, 3:-3, 3:-3, 3:-3]
    advect = sixth_order(lam_ext * vel_ext[0:1], 1, spacings[0])
    for direction in range(1, 3):
        advect = advect + sixth_order(lam_ext * vel_ext[direction:direction + 1], direction + 1, spacings[direction])
    cross_terms = jnp.stack([jnp.sum(lam_block * sixth_order(vel_ext, direction + 1, spacings[direction]), axis=0)
                             for direction in range(3)])
    advect = advect - cross_terms
    return lam_block + time_step * (advect + closure_adj)


def reference(velocity, cotangent, weight_in, bias_in, weight_out):
    spectrum = jnp.fft.fftn(cotangent, axes=(1, 2, 3))
    wave_x = (jnp.fft.fftfreq(NX) * NX)[:, None, None]
    wave_y = (jnp.fft.fftfreq(NY) * NY)[None, :, None]
    wave_z = (jnp.fft.fftfreq(NZ) * NZ)[None, None, :]
    retain = ((wave_x != -(NX // 2)) & (wave_y != -(NY // 2)) & (wave_z != -(NZ // 2)))
    squared = wave_x * wave_x + wave_y * wave_y + wave_z * wave_z
    inverse = jnp.where(squared > 0, 1.0 / jnp.maximum(squared, 1.0), 0.0)
    dotted = (wave_x * spectrum[0] + wave_y * spectrum[1] + wave_z * spectrum[2]) * inverse
    projected = jnp.stack([spectrum[0] - wave_x * dotted,
                           spectrum[1] - wave_y * dotted,
                           spectrum[2] - wave_z * dotted]) * retain[None]
    lam = jnp.real(jnp.fft.ifftn(projected, axes=(1, 2, 3))).astype(jnp.float32)
    widths = ((0, 0), (3, 3), (3, 3), (3, 3))
    vel_pad = jnp.pad(velocity, widths, mode="wrap")
    lam_pad = jnp.pad(lam, widths, mode="wrap")
    spacings = (2.0 * math.pi / NX, 2.0 * math.pi / NY, 2.0 * math.pi / NZ)
    slab_width = math.gcd(NX, 16)
    slab_count = NX // slab_width

    def one_slab(slab_index):
        slab_start = (slab_index * slab_width).astype(jnp.int32)
        vel_slab = lax.dynamic_slice_in_dim(vel_pad, slab_start, slab_width + 6, 1)
        lam_slab = lax.dynamic_slice_in_dim(lam_pad, slab_start, slab_width + 6, 1)
        return step_adjoint(vel_slab, lam_slab, weight_in, bias_in, weight_out, spacings)

    pieces = lax.map(one_slab, jnp.arange(slab_count, dtype=jnp.int32))
    return pieces.transpose(1, 0, 2, 3, 4).reshape(COMP, NX, NY, NZ)
```

```python
import functools
import math

import jax
import jax.numpy as jnp
import numpy as np
from jax import lax
from jax.experimental import pallas as pl
from jax.experimental.pallas import tpu as pltpu
from jax.sharding import PartitionSpec as P

time_step = 0.005
high = lax.Precision.HIGH
LANES = 128
taps = ((1, 45.0), (2, -9.0), (3, 1.0))


def rows_of(ny):
    return -(-(ny + 6) // 8) * 8


def halo(block, axis, dim, width):
    count = lax.axis_size(axis)
    forward = [(i, (i + 1) % count) for i in range(count)]
    backward = [(target, source) for source, target in forward]
    low = lax.ppermute(
        lax.slice_in_dim(block, block.shape[dim] - width, None, axis=dim), axis, forward
    )
    high_side = lax.ppermute(lax.slice_in_dim(block, 0, width, axis=dim), axis, backward)
    return low, high_side


def bordered(block):
    low, up = halo(block, "py", 2, 3)
    ny = block.shape[2]
    extra = rows_of(ny) - ny - 6
    parts = [low, block, up]
    if extra:
        parts.append(jnp.zeros(block.shape[:2] + (extra,) + block.shape[3:], block.dtype))
    wide = jnp.concatenate(parts, axis=2)
    low, up = halo(wide, "px", 1, 3)
    return jnp.concatenate([low, wide, up], axis=1)


def closure_kernel(sizes, vel, lam, w1, b1, w2, w3, out, vs, ss, acc):
    nx, ny, rows, half, spacings = sizes
    vblock, sblock = 9 * rows, 18 * rows
    inv2 = [1.0 / (2.0 * h) for h in spacings]
    inv60 = [1.0 / (60.0 * h) for h in spacings]

    def zroll(value, shift):
        return pltpu.roll(value, shift % LANES, value.ndim - 1)

    def prepare(k, side):
        e = k + 1 + side * half
        lanes = slice(side * LANES, (side + 1) * LANES)
        v = vel[:, e].reshape(3 * rows, LANES)
        l = [lam[c, e] for c in range(3)]
        dx = [(lam[c, e + 1] - lam[c, e - 1]) * inv2[0] for c in range(3)]
        dy = [(pltpu.roll(l[c], rows - 1, 0) - pltpu.roll(l[c], 1, 0)) * inv2[1] for c in range(3)]
        dz = [(zroll(l[c], -1) - zroll(l[c], 1)) * inv2[2] for c in range(3)]
        s = jnp.concatenate(
            [dx[0], dy[1], dz[2], dy[0] + dx[1], dz[0] + dx[2], dz[1] + dy[2]], axis=0
        )
        for t in range(3):
            vs[pl.ds(pl.multiple_of(k * vblock + t * 3 * rows, 8), 3 * rows), lanes] = zroll(
                v, 1 - t
            ).astype(jnp.bfloat16)
            ss[pl.ds(pl.multiple_of(k * sblock + t * 6 * rows, 8), 6 * rows), lanes] = zroll(
                s, 1 - t
            ).astype(jnp.bfloat16)

    @pl.loop(0, half + 2)
    def _(k):
        prepare(k, 0)
        prepare(k, 1)

    acc[...] = jnp.zeros_like(acc)

    def step(i):
        pre = jnp.dot(
            w1[...],
            vs[pl.ds(pl.multiple_of(i * vblock, 16), 3 * vblock), :],
            preferred_element_type=jnp.float32,
        )
        hid = jnp.dot(
            w2[...],
            ss[pl.ds(pl.multiple_of(i * sblock, 16), 3 * sblock), :],
            preferred_element_type=jnp.float32,
        )
        t = jnp.tanh(pre + b1[...])
        p = (hid * (1.0 - t * t)).astype(jnp.bfloat16)
        c = jnp.dot(w3[...], p, preferred_element_type=jnp.float32)
        for d in range(3):
            acc[i + d] += c[d * 9 * ny : (d + 1) * 9 * ny]

    @pl.loop(0, half)
    def _(i):
        step(i)

    for d in range(2):
        acc[half + d, :, :LANES] += acc[d, :, LANES:]

    def finish(x, idx, side):
        e = x + 3
        lanes = slice(side * LANES, (side + 1) * LANES)
        low = [acc[idx, d * 3 * ny : (d + 1) * 3 * ny, lanes] for d in range(3)]
        closure = zroll(low[0], -1) + low[1] + zroll(low[2], 1)
        mid = slice(3, 3 + ny)
        l0 = [lam[c, e, mid] for c in range(3)]
        v0 = [vel[c, e, mid] for c in range(3)]
        total = [closure[c * ny : (c + 1) * ny] for c in range(3)]
        lz = [l0[c] * v0[2] for c in range(3)]
        for b in range(3):
            grad_flux = [0.0] * 3
            grad_vel = [0.0] * 3
            for d, weight in taps:
                for sign in (1, -1):
                    q = d * sign
                    if b == 0:
                        vq = [vel[c, e + q, mid] for c in range(3)]
                        fq = [lam[c, e + q, mid] * vq[0] for c in range(3)]
                    elif b == 1:
                        ys = slice(3 + q, 3 + q + ny)
                        vq = [vel[c, e, ys] for c in range(3)]
                        fq = [lam[c, e, ys] * vq[1] for c in range(3)]
                    else:
                        vq = [zroll(v0[c], -q) for c in range(3)]
                        fq = [zroll(lz[c], -q) for c in range(3)]
                    w = weight * sign * inv60[b]
                    for c in range(3):
                        grad_flux[c] += w * fq[c]
                        grad_vel[c] += w * vq[c]
            for c in range(3):
                total[c] += grad_flux[c]
            total[b] -= l0[0] * grad_vel[0] + l0[1] * grad_vel[1] + l0[2] * grad_vel[2]
        for c in range(3):
            out[c, x] = l0[c] + time_step * total[c]

    @pl.loop(0, half)
    def _(x):
        finish(x, x + 2, 0)

    @pl.loop(half, nx)
    def _(x):
        finish(x, x + 2 - half, 1)


def band(ny, rows, first):
    table = np.zeros((ny, 3, rows), np.float32)
    for y in range(ny):
        for d in range(3):
            table[y, d, y + d + first] = 1.0
    return jnp.asarray(table, jnp.bfloat16)


def closure_weights(weight_in, bias_in, weight_out, ny, rows):
    hid = weight_in.shape[0]
    w1 = jnp.einsum("ocxyz,pyq->opxzcq", weight_in, band(ny + 2, rows, 1))
    w1 = w1.reshape(hid * (ny + 2), 27 * rows)
    flipped = jnp.flip(weight_out, (2, 3, 4))
    w2 = jnp.einsum("ocxyz,pyq->cpxzoq", flipped, band(ny + 2, rows, 1))
    w2 = w2.reshape(hid * (ny + 2), 54 * rows)
    back = jnp.flip(band(ny, ny + 2, 0), 1)
    w3 = jnp.einsum("ocxyz,pyq->xzcpoq", weight_in, back)
    w3 = w3.reshape(27 * ny, hid * (ny + 2))
    bias = jnp.broadcast_to(bias_in[:, None], (hid, ny + 2)).reshape(hid * (ny + 2), 1)
    return w1, bias, w2, w3


def closure_step(vel_ext, lam_ext, weights, nx, ny, spacings):
    rows = vel_ext.shape[2]
    half = (nx + 2) // 2
    w1, bias, w2, w3 = weights
    kernel = functools.partial(closure_kernel, (nx, ny, rows, half, spacings))
    vm = pl.BlockSpec(memory_space=pltpu.VMEM)
    return pl.pallas_call(
        kernel,
        out_shape=jax.ShapeDtypeStruct((3, nx, ny, LANES), jnp.float32),
        in_specs=[vm] * 6,
        out_specs=vm,
        scratch_shapes=[
            pltpu.VMEM(((half + 2) * 9 * rows, 2 * LANES), jnp.bfloat16),
            pltpu.VMEM(((half + 2) * 18 * rows, 2 * LANES), jnp.bfloat16),
            pltpu.VMEM((half + 2, 9 * ny, 2 * LANES), jnp.float32),
        ],
        compiler_params=pltpu.CompilerParams(vmem_limit_bytes=50 * 2**20),
        name="closure",
    )(vel_ext, lam_ext, w1, bias, w2, w3)


def waves(length, modes):
    products = np.arange(length)[:, None] * np.arange(modes)[None, :] % length
    phases = products.astype(np.float64) * (2.0 * math.pi / length)
    return np.cos(phases), np.sin(phases)


def f32(table):
    return jnp.asarray(np.asarray(table, np.float32))


def project(re, im, index_x, index_y, index_z, sizes):
    NX, NY, NZ = sizes

    def signed(index, length):
        return jnp.where(index > length // 2, index - length, index).astype(jnp.float32)

    wx, wy, wz = signed(index_x, NX), signed(index_y, NY), signed(index_z, NZ)
    squared = wx * wx + wy * wy + wz * wz
    keep = (index_x != NX // 2) & (index_y != NY // 2) & (index_z != NZ // 2)
    inverse = jnp.where(squared > 0, 1.0 / jnp.maximum(squared, 1.0), 0.0)
    done = []
    for part in (re, im):
        dotted = (wx * part[0] + wy * part[1] + wz * part[2]) * inverse
        done.append([jnp.where(keep, part[c] - w * dotted, 0.0) for c, w in enumerate((wx, wy, wz))])
    return jnp.stack(done[0]), jnp.stack(done[1])


def einsum(*args):
    return jnp.einsum(*args, precision=high)


def mode_weights(NX, NY, NZ):
    scale = np.full((NZ // 2,), 2.0 / (NX * NY * NZ))
    scale[0] /= 2.0
    return scale


def projected_once(cotangent, sizes, npx, npy):
    NX, NY, NZ = sizes
    _, nx, ny, _ = cotangent.shape
    total = npx * npy
    nj = NZ // 2 // total
    cz, sz = waves(NZ, NZ // 2)
    cy, sy = waves(NY, NY)
    cx, sx = waves(NX, NX)
    forward_z = np.stack([cz, -sz], axis=1).reshape(NZ, 2, total, nj)
    sent = einsum("cxyz,zrdj->drcyjx", cotangent, f32(forward_z))
    sent = sent.reshape(total, 2 * 3 * ny, nj * nx)
    got = lax.all_to_all(sent, ("px", "py"), 0, 0, tiled=True)
    got = got.reshape(npx, npy, 2, 3, ny, nj, nx)
    forward_y = np.stack([np.stack([cy, -sy], 0), np.stack([sy, cy], 0)], 0)
    forward_y = forward_y.reshape(2, 2, npy, ny, NY)
    mixed = einsum("hprcyjx,rRpyl->Rcljhx", got, f32(forward_y))
    mixed = mixed.reshape(2, 3, NY, nj, NX)
    trans = einsum("Rcljx,xSm->SRcljm", mixed, f32(np.stack([cx, sx], 1)))
    re = trans[0, 0] + trans[1, 1]
    im = trans[0, 1] - trans[1, 0]
    me = lax.axis_index("px") * npy + lax.axis_index("py")
    index_z = (me * nj + jnp.arange(nj, dtype=jnp.int32))[None, :, None]
    index_y = jnp.arange(NY, dtype=jnp.int32)[:, None, None]
    index_x = jnp.arange(NX, dtype=jnp.int32)[None, None, :]
    re, im = project(re, im, index_x, index_y, index_z, sizes)
    back = einsum("Rcljm,mSx->SRcljx", jnp.stack([re, im]), f32(np.stack([cx, sx], 1)))
    re = back[0, 0] - back[1, 1]
    im = back[1, 0] + back[0, 1]
    inverse_y = np.stack([np.stack([cy, sy], 0), np.stack([-sy, cy], 0)], 0)
    inverse_y = inverse_y.reshape(2, 2, NY, npy, ny)
    sent = einsum(
        "Rcljhx,Rrlpy->hprcyjx",
        jnp.stack([re, im]).reshape(2, 3, NY, nj, npx, nx),
        f32(inverse_y),
    ).reshape(total, 2 * 3 * ny, nj * nx)
    got = lax.all_to_all(sent, ("px", "py"), 0, 0, tiled=True)
    got = got.reshape(total, 2, 3, ny, nj, nx)
    scale = mode_weights(NX, NY, NZ)
    inverse_z = np.stack([(cz * scale).T, (-sz * scale).T], 0).reshape(2, total, nj, NZ)
    return einsum("drcyjx,rdjz->cxyz", got, f32(inverse_z))


def projected_twice(cotangent, sizes, npx, npy):
    NX, NY, NZ = sizes
    cz, sz = waves(NZ, NZ // 2)
    cy, sy = map(f32, waves(NY, NY))
    cx, sx = map(f32, waves(NX, NX))
    scale = mode_weights(NX, NY, NZ)
    stacked = jnp.stack(
        [einsum("cxyz,zk->cxyk", cotangent, f32(cz)), einsum("cxyz,zk->cxyk", cotangent, f32(-sz))]
    )
    re, im = lax.all_to_all(stacked, "py", split_axis=4, concat_axis=3, tiled=True)
    pair = jnp.stack(
        [
            einsum("cxyk,yl->ckxl", re, cy) + einsum("cxyk,yl->ckxl", im, sy),
            einsum("cxyk,yl->ckxl", im, cy) - einsum("cxyk,yl->ckxl", re, sy),
        ]
    )
    re, im = lax.all_to_all(pair, "px", split_axis=4, concat_axis=3, tiled=True)
    re, im = (
        einsum("ckxl,xm->cklm", re, cx) + einsum("ckxl,xm->cklm", im, sx),
        einsum("ckxl,xm->cklm", im, cx) - einsum("ckxl,xm->cklm", re, sx),
    )
    nk, nl = re.shape[1], re.shape[2]
    index_z = (lax.axis_index("py") * nk + jnp.arange(nk, dtype=jnp.int32))[:, None, None]
    index_y = (lax.axis_index("px") * nl + jnp.arange(nl, dtype=jnp.int32))[None, :, None]
    index_x = jnp.arange(NX, dtype=jnp.int32)[None, None, :]
    re, im = project(re, im, index_x, index_y, index_z, sizes)
    pair = jnp.stack(
        [
            einsum("cklm,mx->ckxl", re, cx) - einsum("cklm,mx->ckxl", im, sx),
            einsum("cklm,mx->ckxl", re, sx) + einsum("cklm,mx->ckxl", im, cx),
        ]
    )
    re, im = lax.all_to_all(pair, "px", split_axis=3, concat_axis=4, tiled=True)
    pair = jnp.stack(
        [
            einsum("ckxl,ly->cxyk", re, cy) - einsum("ckxl,ly->cxyk", im, sy),
            einsum("ckxl,ly->cxyk", re, sy) + einsum("ckxl,ly->cxyk", im, cy),
        ]
    )
    re, im = lax.all_to_all(pair, "py", split_axis=3, concat_axis=4, tiled=True)
    return einsum("cxyk,kz->cxyz", re, f32((cz * scale).T)) - einsum(
        "cxyk,kz->cxyz", im, f32((sz * scale).T)
    )


def body(velocity, cotangent, weight_in, bias_in, weight_out):
    npx, npy = lax.axis_size("px"), lax.axis_size("py")
    _, nx, ny, NZ = velocity.shape
    sizes = (nx * npx, ny * npy, NZ)
    spacings = tuple(2.0 * math.pi / size for size in sizes)
    vel_ext = bordered(velocity)
    weights = closure_weights(weight_in, bias_in, weight_out, ny, rows_of(ny))
    if (NZ // 2) % (npx * npy) == 0:
        lam = projected_once(cotangent, sizes, npx, npy)
    else:
        lam = projected_twice(cotangent, sizes, npx, npy)
    lam_ext = bordered(lam)
    return closure_step(vel_ext, lam_ext, weights, nx, ny, spacings)


def solution(mesh):
    placed = (P(None, "px", "py", None), P(None, "px", "py", None), P(), P(), P())
    return jax.shard_map(
        body, mesh=mesh, in_specs=placed, out_specs=P(None, "px", "py", None), check_vma=False
    )
```

```python
import functools
import math

import jax
import jax.numpy as jnp
import numpy as np
from jax import lax
from jax.experimental import pallas as pl
from jax.experimental.pallas import tpu as pltpu
from jax.sharding import PartitionSpec as P

time_step = 0.005
high = lax.Precision.HIGH
LANES = 128
taps = ((1, 45.0), (2, -9.0), (3, 1.0))


def rows_of(ny):
    return -(-(ny + 6) // 8) * 8


def halo(block, axis, dim, width):
    count = lax.axis_size(axis)
    forward = [(i, (i + 1) % count) for i in range(count)]
    backward = [(target, source) for source, target in forward]
    low = lax.ppermute(
        lax.slice_in_dim(block, block.shape[dim] - width, None, axis=dim), axis, forward
    )
    high_side = lax.ppermute(lax.slice_in_dim(block, 0, width, axis=dim), axis, backward)
    return low, high_side


def bordered(block):
    low, up = halo(block, "py", 2, 3)
    ny = block.shape[2]
    extra = rows_of(ny) - ny - 6
    parts = [low, block, up]
    if extra:
        parts.append(jnp.zeros(block.shape[:2] + (extra,) + block.shape[3:], block.dtype))
    wide = jnp.concatenate(parts, axis=2)
    low, up = halo(wide, "px", 1, 3)
    return jnp.concatenate([low, wide, up], axis=1)


def zroll(value, shift):
    return pltpu.roll(value, shift % LANES, value.ndim - 1)


def many(count, size, run):
    if count % size:
        size = 1

    @pl.loop(0, count // size)
    def _(block):
        for piece in range(size):
            run(block * size + piece)


def velocity_kernel(sizes, vel, w1, b1, slope, grads, vs):
    nx, ny, rows, half, spacings = sizes
    vblock, out_rows = 9 * rows, w1.shape[0]

    def prepare(k):
        for side in range(2):
            v = vel[:, k + 1 + side * half].reshape(3 * rows, LANES)
            for t in range(3):
                start = pl.multiple_of(k * vblock + t * 3 * rows, 16)
                vs[pl.ds(start, 3 * rows), side * LANES : (side + 1) * LANES] = zroll(
                    v, 1 - t
                ).astype(jnp.bfloat16)

    many(half + 2, 5, prepare)

    def step(i):
        pre = jnp.dot(
            w1[:, : 3 * vblock],
            vs[pl.ds(pl.multiple_of(i * vblock, 16), 3 * vblock), :],
            preferred_element_type=jnp.float32,
        )
        t = jnp.tanh(pre + b1[...])
        slope[pl.ds(pl.multiple_of(i * out_rows, 16), out_rows), :] = (1.0 - t * t).astype(
            jnp.bfloat16
        )

    many(half, 3, step)

    def gradient(x):
        e = x + 3
        mid = slice(3, 3 + ny)
        for c in range(3):
            v0 = vel[c, e, mid]
            for b in range(3):
                total = 0.0
                for d, weight in taps:
                    if b == 0:
                        pair = vel[c, e + d, mid] - vel[c, e - d, mid]
                    elif b == 1:
                        pair = vel[c, e, 3 + d : 3 + d + ny] - vel[c, e, 3 - d : 3 - d + ny]
                    else:
                        pair = zroll(v0, -d) - zroll(v0, d)
                    total += (weight / (60.0 * spacings[b])) * pair
                grads[3 * b + c, x] = total

    many(nx, 2, gradient)


def closure_kernel(sizes, vel, lam, slope, grads, w2, w3, out, ss, acc):
    nx, ny, rows, half, spacings = sizes
    sblock, hid_rows = 18 * rows, w2.shape[0]
    inv2 = [1.0 / (2.0 * h) for h in spacings]

    def prepare(k):
        for side in range(2):
            e = k + 1 + side * half
            lanes = slice(side * LANES, (side + 1) * LANES)
            l = [lam[c, e] for c in range(3)]
            dx = [(lam[c, e + 1] - lam[c, e - 1]) * inv2[0] for c in range(3)]
            dy = [
                (pltpu.roll(l[c], rows - 1, 0) - pltpu.roll(l[c], 1, 0)) * inv2[1]
                for c in range(3)
            ]
            dz = [(zroll(l[c], -1) - zroll(l[c], 1)) * inv2[2] for c in range(3)]
            s = jnp.concatenate(
                [dx[0], dy[1], dz[2], dy[0] + dx[1], dz[0] + dx[2], dz[1] + dy[2]], axis=0
            )
            for t in range(3):
                start = pl.multiple_of(k * sblock + t * 6 * rows, 16)
                ss[pl.ds(start, 6 * rows), lanes] = zroll(s, 1 - t).astype(jnp.bfloat16)
        acc[k] = jnp.zeros(acc.shape[1:], acc.dtype)

    many(half + 2, 5, prepare)

    def step(i):
        hid = jnp.dot(
            w2[:, : 3 * sblock],
            ss[pl.ds(pl.multiple_of(i * sblock, 16), 3 * sblock), :],
            preferred_element_type=jnp.float32,
        )
        part = slope[pl.ds(pl.multiple_of(i * hid_rows, 16), hid_rows), :]
        p = (hid * part.astype(jnp.float32)).astype(jnp.bfloat16)
        c = jnp.dot(w3[...], p, preferred_element_type=jnp.float32)
        for d in range(3):
            acc[i + d] += c[d * 9 * ny : (d + 1) * 9 * ny]

    many(half, 3, step)

    for d in range(2):
        acc[half + d, :, :LANES] += acc[d, :, LANES:]

    def finish(x, idx, side):
        e = x + 3
        lanes = slice(side * LANES, (side + 1) * LANES)
        low = [acc[idx, d * 3 * ny : (d + 1) * 3 * ny, lanes] for d in range(3)]
        closure = zroll(low[0], -1) + low[1] + zroll(low[2], 1)
        mid = slice(3, 3 + ny)
        l0 = [lam[c, e, mid] for c in range(3)]
        vz = vel[2, e, mid]
        for c in range(3):
            total = closure[c * ny : (c + 1) * ny]
            lz = l0[c] * vz
            for d, weight in taps:
                fx = lam[c, e + d, mid] * vel[0, e + d, mid] - lam[c, e - d, mid] * vel[0, e - d, mid]
                up, down = slice(3 + d, 3 + d + ny), slice(3 - d, 3 - d + ny)
                fy = lam[c, e, up] * vel[1, e, up] - lam[c, e, down] * vel[1, e, down]
                fz = zroll(lz, -d) - zroll(lz, d)
                for b, pair in enumerate((fx, fy, fz)):
                    total += (weight / (60.0 * spacings[b])) * pair
            for a in range(3):
                total -= l0[a] * grads[3 * c + a, x]
            out[c, x] = l0[c] + time_step * total

    many(half, 3, lambda x: finish(x, x + 2, 0))
    many(nx - half, 2, lambda x: finish(x + half, x + 2, 1))


def lane_padded(size):
    return -(-size // LANES) * LANES


def banded_table(channels, ny, rows):
    table = np.zeros((channels, 3, 3, 3, ny + 2, 3, 3, channels, rows), np.float32)
    for c in range(channels):
        for x in range(3):
            for d in range(3):
                for z in range(3):
                    for p in range(ny + 2):
                        table[c, x, d, z, p, x, z, c, p + d + 1] = 1.0
    table = table.reshape(27 * channels, ny + 2, 9 * channels * rows)
    extra = lane_padded(table.shape[2]) - table.shape[2]
    return np.pad(table, ((0, 0), (0, 0), (0, extra)))


def returned_table(channels, ny):
    table = np.zeros((channels, 3, 3, 3, ny + 2, 3, 3, channels, ny), np.float32)
    for c in range(channels):
        for x in range(3):
            for d in range(3):
                for z in range(3):
                    for y in range(ny):
                        table[c, x, d, z, y + 2 - d, x, z, c, y] = 1.0
    table = table.reshape(27 * channels, ny + 2, 9 * channels * ny)
    extra = lane_padded(table.shape[2]) - table.shape[2]
    return np.pad(table, ((0, 0), (0, 0), (0, extra)))


def spread(weight, table):
    flat = table.reshape(table.shape[0], -1)
    wide = jnp.dot(
        weight, jnp.asarray(flat, jnp.bfloat16), preferred_element_type=jnp.float32
    ).astype(jnp.bfloat16)
    columns = table.shape[2]
    return jnp.concatenate(
        [wide[:, p * columns : (p + 1) * columns] for p in range(table.shape[1])], axis=0
    )


def input_weights(weight_in, bias_in, ny, rows):
    hid, comp = weight_in.shape[:2]
    w1 = spread(weight_in.reshape(hid, -1), banded_table(comp, ny, rows))
    return w1, jnp.tile(bias_in, ny + 2)[:, None]


def output_weights(weight_in, weight_out, ny, rows):
    hid, comp = weight_in.shape[:2]
    flipped = jnp.flip(weight_out, (2, 3, 4)).transpose(1, 0, 2, 3, 4).reshape(hid, -1)
    w2 = spread(flipped, banded_table(weight_out.shape[0], ny, rows))
    w3 = spread(weight_in.reshape(hid, -1), returned_table(comp, ny)).T[: 9 * comp * ny]
    return w2, w3


def velocity_step(vel_ext, w1, bias, nx, ny, spacings):
    rows = vel_ext.shape[2]
    half = (nx + 2) // 2
    vm = pl.BlockSpec(memory_space=pltpu.VMEM)
    return pl.pallas_call(
        functools.partial(velocity_kernel, (nx, ny, rows, half, spacings)),
        out_shape=(
            jax.ShapeDtypeStruct((half * w1.shape[0], 2 * LANES), jnp.bfloat16),
            jax.ShapeDtypeStruct((9, nx, ny, LANES), jnp.float32),
        ),
        in_specs=[vm] * 3,
        out_specs=(vm, vm),
        scratch_shapes=[pltpu.VMEM(((half + 2) * 9 * rows, 2 * LANES), jnp.bfloat16)],
        compiler_params=pltpu.CompilerParams(vmem_limit_bytes=40 * 2**20),
        cost_estimate=pl.CostEstimate(
            flops=2 * half * w1.shape[0] * w1.shape[1] * 2 * LANES,
            bytes_accessed=12 * 2**20,
            transcendentals=half * w1.shape[0] * 2 * LANES,
        ),
        name="velocity",
    )(vel_ext, w1, bias)


def closure_step(vel_ext, lam_ext, slope, grads, w2, w3, nx, ny, spacings):
    rows = vel_ext.shape[2]
    half = (nx + 2) // 2
    vm = pl.BlockSpec(memory_space=pltpu.VMEM)
    return pl.pallas_call(
        functools.partial(closure_kernel, (nx, ny, rows, half, spacings)),
        out_shape=jax.ShapeDtypeStruct((3, nx, ny, LANES), jnp.float32),
        in_specs=[vm] * 6,
        out_specs=vm,
        scratch_shapes=[
            pltpu.VMEM(((half + 2) * 18 * rows, 2 * LANES), jnp.bfloat16),
            pltpu.VMEM((half + 2, 9 * ny, 2 * LANES), jnp.float32),
        ],
        compiler_params=pltpu.CompilerParams(vmem_limit_bytes=50 * 2**20),
        name="closure",
    )(vel_ext, lam_ext, slope, grads, w2, w3)


def waves(length, modes):
    products = np.arange(length)[:, None] * np.arange(modes)[None, :] % length
    phases = products.astype(np.float64) * (2.0 * math.pi / length)
    return np.cos(phases), np.sin(phases)


def f32(table):
    return jnp.asarray(np.asarray(table, np.float32))


def project(re, im, index_x, index_y, index_z, sizes):
    NX, NY, NZ = sizes

    def signed(index, length):
        return jnp.where(index > length // 2, index - length, index).astype(jnp.float32)

    wx, wy, wz = signed(index_x, NX), signed(index_y, NY), signed(index_z, NZ)
    squared = wx * wx + wy * wy + wz * wz
    keep = (index_x != NX // 2) & (index_y != NY // 2) & (index_z != NZ // 2)
    inverse = jnp.where(squared > 0, 1.0 / jnp.maximum(squared, 1.0), 0.0)
    done = []
    for part in (re, im):
        dotted = (wx * part[0] + wy * part[1] + wz * part[2]) * inverse
        done.append([jnp.where(keep, part[c] - w * dotted, 0.0) for c, w in enumerate((wx, wy, wz))])
    return jnp.stack(done[0]), jnp.stack(done[1])


def einsum(*args):
    return jnp.einsum(*args, precision=high)


def mode_weights(NX, NY, NZ):
    scale = np.full((NZ // 2,), 2.0 / (NX * NY * NZ))
    scale[0] /= 2.0
    return scale


def projected_once(cotangent, sizes, npx, npy, others, beside_first, beside_second):
    NX, NY, NZ = sizes
    _, nx, ny, _ = cotangent.shape
    total = npx * npy
    nj = NZ // 2 // total
    cz, sz = waves(NZ, NZ // 2)
    cy, sy = waves(NY, NY)
    cx, sx = waves(NX, NX)
    forward_z = np.stack([cz, -sz], axis=1).reshape(NZ, 2, total, nj)
    sent = einsum("cxyz,zrdj->drcyjx", cotangent, f32(forward_z))
    sent = sent.reshape(total, 2 * 3 * ny, nj * nx)
    sent, others = lax.optimization_barrier((sent, others))
    got = lax.all_to_all(sent, ("px", "py"), 0, 0, tiled=True)
    got, first = lax.optimization_barrier((got, beside_first(*others)))
    got = got.reshape(npx, npy, 2, 3, ny, nj, nx)
    forward_y = np.stack([np.stack([cy, -sy], 0), np.stack([sy, cy], 0)], 0)
    forward_y = forward_y.reshape(2, 2, npy, ny, NY)
    mixed = einsum("hprcyjx,rRpyl->Rcljhx", got, f32(forward_y))
    mixed = mixed.reshape(2, 3, NY, nj, NX)
    trans = einsum("Rcljx,xSm->SRcljm", mixed, f32(np.stack([cx, sx], 1)))
    re = trans[0, 0] + trans[1, 1]
    im = trans[0, 1] - trans[1, 0]
    me = lax.axis_index("px") * npy + lax.axis_index("py")
    index_z = (me * nj + jnp.arange(nj, dtype=jnp.int32))[None, :, None]
    index_y = jnp.arange(NY, dtype=jnp.int32)[:, None, None]
    index_x = jnp.arange(NX, dtype=jnp.int32)[None, None, :]
    re, im = project(re, im, index_x, index_y, index_z, sizes)
    back = einsum("Rcljm,mSx->SRcljx", jnp.stack([re, im]), f32(np.stack([cx, sx], 1)))
    re = back[0, 0] - back[1, 1]
    im = back[1, 0] + back[0, 1]
    inverse_y = np.stack([np.stack([cy, sy], 0), np.stack([-sy, cy], 0)], 0)
    inverse_y = inverse_y.reshape(2, 2, NY, npy, ny)
    sent = einsum(
        "Rcljhx,Rrlpy->hprcyjx",
        jnp.stack([re, im]).reshape(2, 3, NY, nj, npx, nx),
        f32(inverse_y),
    ).reshape(total, 2 * 3 * ny, nj * nx)
    sent, first = lax.optimization_barrier((sent, first))
    got = lax.all_to_all(sent, ("px", "py"), 0, 0, tiled=True)
    got, second = lax.optimization_barrier((got, beside_second(first)))
    got = got.reshape(total, 2, 3, ny, nj, nx)
    scale = mode_weights(NX, NY, NZ)
    inverse_z = np.stack([(cz * scale).T, (-sz * scale).T], 0).reshape(2, total, nj, NZ)
    return einsum("drcyjx,rdjz->cxyz", got, f32(inverse_z)), second


def projected_twice(cotangent, sizes, npx, npy):
    NX, NY, NZ = sizes
    cz, sz = waves(NZ, NZ // 2)
    cy, sy = map(f32, waves(NY, NY))
    cx, sx = map(f32, waves(NX, NX))
    scale = mode_weights(NX, NY, NZ)
    stacked = jnp.stack(
        [einsum("cxyz,zk->cxyk", cotangent, f32(cz)), einsum("cxyz,zk->cxyk", cotangent, f32(-sz))]
    )
    re, im = lax.all_to_all(stacked, "py", split_axis=4, concat_axis=3, tiled=True)
    pair = jnp.stack(
        [
            einsum("cxyk,yl->ckxl", re, cy) + einsum("cxyk,yl->ckxl", im, sy),
            einsum("cxyk,yl->ckxl", im, cy) - einsum("cxyk,yl->ckxl", re, sy),
        ]
    )
    re, im = lax.all_to_all(pair, "px", split_axis=4, concat_axis=3, tiled=True)
    re, im = (
        einsum("ckxl,xm->cklm", re, cx) + einsum("ckxl,xm->cklm", im, sx),
        einsum("ckxl,xm->cklm", im, cx) - einsum("ckxl,xm->cklm", re, sx),
    )
    nk, nl = re.shape[1], re.shape[2]
    index_z = (lax.axis_index("py") * nk + jnp.arange(nk, dtype=jnp.int32))[:, None, None]
    index_y = (lax.axis_index("px") * nl + jnp.arange(nl, dtype=jnp.int32))[None, :, None]
    index_x = jnp.arange(NX, dtype=jnp.int32)[None, None, :]
    re, im = project(re, im, index_x, index_y, index_z, sizes)
    pair = jnp.stack(
        [
            einsum("cklm,mx->ckxl", re, cx) - einsum("cklm,mx->ckxl", im, sx),
            einsum("cklm,mx->ckxl", re, sx) + einsum("cklm,mx->ckxl", im, cx),
        ]
    )
    re, im = lax.all_to_all(pair, "px", split_axis=3, concat_axis=4, tiled=True)
    pair = jnp.stack(
        [
            einsum("ckxl,ly->cxyk", re, cy) - einsum("ckxl,ly->cxyk", im, sy),
            einsum("ckxl,ly->cxyk", re, sy) + einsum("ckxl,ly->cxyk", im, cy),
        ]
    )
    re, im = lax.all_to_all(pair, "py", split_axis=3, concat_axis=4, tiled=True)
    return einsum("cxyk,kz->cxyz", re, f32((cz * scale).T)) - einsum(
        "cxyk,kz->cxyz", im, f32((sz * scale).T)
    )


def body(velocity, cotangent, weight_in, bias_in, weight_out):
    npx, npy = lax.axis_size("px"), lax.axis_size("py")
    _, nx, ny, NZ = velocity.shape
    sizes = (nx * npx, ny * npy, NZ)
    spacings = tuple(2.0 * math.pi / size for size in sizes)
    rows = rows_of(ny)

    def beside_first(velocity, weight_in, bias_in, weight_out):
        w1, bias = input_weights(weight_in, bias_in, ny, rows)
        w2, w3 = output_weights(weight_in, weight_out, ny, rows)
        return bordered(velocity), w1, bias, w2, w3

    def beside_second(first):
        vel_ext, w1, bias, w2, w3 = first
        slope, grads = velocity_step(vel_ext, w1, bias, nx, ny, spacings)
        return vel_ext, slope, grads, w2, w3

    others = (velocity, weight_in, bias_in, weight_out)
    if (NZ // 2) % (npx * npy) == 0:
        lam, second = projected_once(cotangent, sizes, npx, npy, others, beside_first, beside_second)
    else:
        lam = projected_twice(cotangent, sizes, npx, npy)
        second = beside_second(beside_first(*others))
    vel_ext, slope, grads, w2, w3 = second
    return closure_step(vel_ext, bordered(lam), slope, grads, w2, w3, nx, ny, spacings)


def solution(mesh):
    placed = (P(None, "px", "py", None), P(None, "px", "py", None), P(), P(), P())
    return jax.shard_map(
        body, mesh=mesh, in_specs=placed, out_specs=P(None, "px", "py", None), check_vma=False
    )
```

```python
import functools
import math

import jax
import jax.numpy as jnp
import ml_dtypes
import numpy as np
from jax import lax
from jax.experimental import pallas as pl
from jax.experimental.pallas import tpu as pltpu
from jax.sharding import PartitionSpec as P

time_step = 0.005
high = lax.Precision.HIGH
LANES = 128
taps = ((1, 45.0), (2, -9.0), (3, 1.0))


def rows_of(ny):
    return -(-(ny + 6) // 8) * 8


def halo(block, axis, dim, width):
    count = lax.axis_size(axis)
    forward = [(i, (i + 1) % count) for i in range(count)]
    backward = [(target, source) for source, target in forward]
    low = lax.ppermute(
        lax.slice_in_dim(block, block.shape[dim] - width, None, axis=dim), axis, forward
    )
    high_side = lax.ppermute(lax.slice_in_dim(block, 0, width, axis=dim), axis, backward)
    return low, high_side


def bordered(block):
    return bordered_rest(block, *halo(block, "py", 2, 3))


def bordered_rest(block, low, up):
    ny = block.shape[2]
    extra = rows_of(ny) - ny - 6
    parts = [low, block, up]
    if extra:
        parts.append(jnp.zeros(block.shape[:2] + (extra,) + block.shape[3:], block.dtype))
    wide = jnp.concatenate(parts, axis=2)
    low, up = halo(wide, "px", 1, 3)
    return jnp.concatenate([low, wide, up], axis=1)


def zroll(value, shift):
    return pltpu.roll(value, shift % LANES, value.ndim - 1)


def many(count, size, run):
    if count % size:
        size = 1

    @pl.loop(0, count // size)
    def _(block):
        for piece in range(size):
            run(block * size + piece)


def velocity_kernel(sizes, vel, w1, b1, slope, grads, vs):
    nx, ny, rows, half, spacings = sizes
    vblock, out_rows = 9 * rows, w1.shape[0]

    def prepare(k):
        for side in range(2):
            v = vel[:, k + 1 + side * half].reshape(3 * rows, LANES)
            for t in range(3):
                start = pl.multiple_of(k * vblock + t * 3 * rows, 16)
                vs[pl.ds(start, 3 * rows), side * LANES : (side + 1) * LANES] = zroll(
                    v, 1 - t
                ).astype(jnp.bfloat16)

    many(half + 2, 5, prepare)

    def step(i):
        pre = jnp.dot(
            w1[:, : 3 * vblock],
            vs[pl.ds(pl.multiple_of(i * vblock, 16), 3 * vblock), :],
            preferred_element_type=jnp.float32,
        )
        t = jnp.tanh(pre + b1[...])
        slope[pl.ds(pl.multiple_of(i * out_rows, 16), out_rows), :] = (1.0 - t * t).astype(
            jnp.bfloat16
        )

    many(half, 3, step)

    def gradient(x):
        e = x + 3
        mid = slice(3, 3 + ny)
        for c in range(3):
            v0 = vel[c, e, mid]
            for b in range(3):
                total = 0.0
                for d, weight in taps:
                    if b == 0:
                        pair = vel[c, e + d, mid] - vel[c, e - d, mid]
                    elif b == 1:
                        pair = vel[c, e, 3 + d : 3 + d + ny] - vel[c, e, 3 - d : 3 - d + ny]
                    else:
                        pair = zroll(v0, -d) - zroll(v0, d)
                    total += (weight / (60.0 * spacings[b])) * pair
                grads[3 * b + c, x] = total

    many(nx, 2, gradient)


def closure_kernel(sizes, vel, lam, slope, grads, w2, w3, out, ss, acc):
    nx, ny, rows, half, spacings = sizes
    sblock, hid_rows = 18 * rows, w2.shape[0]
    inv2 = [1.0 / (2.0 * h) for h in spacings]

    def prepare(k):
        for side in range(2):
            e = k + 1 + side * half
            lanes = slice(side * LANES, (side + 1) * LANES)
            l = [lam[c, e] for c in range(3)]
            dx = [(lam[c, e + 1] - lam[c, e - 1]) * inv2[0] for c in range(3)]
            dy = [
                (pltpu.roll(l[c], rows - 1, 0) - pltpu.roll(l[c], 1, 0)) * inv2[1]
                for c in range(3)
            ]
            dz = [(zroll(l[c], -1) - zroll(l[c], 1)) * inv2[2] for c in range(3)]
            s = jnp.concatenate(
                [dx[0], dy[1], dz[2], dy[0] + dx[1], dz[0] + dx[2], dz[1] + dy[2]], axis=0
            )
            for t in range(3):
                start = pl.multiple_of(k * sblock + t * 6 * rows, 16)
                ss[pl.ds(start, 6 * rows), lanes] = zroll(s, 1 - t).astype(jnp.bfloat16)
        acc[k] = jnp.zeros(acc.shape[1:], acc.dtype)

    many(half + 2, 5, prepare)

    def step(i):
        hid = jnp.dot(
            w2[:, : 3 * sblock],
            ss[pl.ds(pl.multiple_of(i * sblock, 16), 3 * sblock), :],
            preferred_element_type=jnp.float32,
        )
        part = slope[pl.ds(pl.multiple_of(i * hid_rows, 16), hid_rows), :]
        p = (hid * part.astype(jnp.float32)).astype(jnp.bfloat16)
        c = jnp.dot(w3[...], p, preferred_element_type=jnp.float32)
        for d in range(3):
            acc[i + d] += c[d * 9 * ny : (d + 1) * 9 * ny]

    many(half, 3, step)

    for d in range(2):
        acc[half + d, :, :LANES] += acc[d, :, LANES:]

    def finish(x, idx, side):
        e = x + 3
        lanes = slice(side * LANES, (side + 1) * LANES)
        low = [acc[idx, d * 3 * ny : (d + 1) * 3 * ny, lanes] for d in range(3)]
        closure = zroll(low[0], -1) + low[1] + zroll(low[2], 1)
        mid = slice(3, 3 + ny)
        l0 = [lam[c, e, mid] for c in range(3)]
        vz = vel[2, e, mid]
        for c in range(3):
            total = closure[c * ny : (c + 1) * ny]
            lz = l0[c] * vz
            for d, weight in taps:
                fx = lam[c, e + d, mid] * vel[0, e + d, mid] - lam[c, e - d, mid] * vel[0, e - d, mid]
                up, down = slice(3 + d, 3 + d + ny), slice(3 - d, 3 - d + ny)
                fy = lam[c, e, up] * vel[1, e, up] - lam[c, e, down] * vel[1, e, down]
                fz = zroll(lz, -d) - zroll(lz, d)
                for b, pair in enumerate((fx, fy, fz)):
                    total += (weight / (60.0 * spacings[b])) * pair
            for a in range(3):
                total -= l0[a] * grads[3 * c + a, x]
            out[c, x] = l0[c] + time_step * total

    many(half, 3, lambda x: finish(x, x + 2, 0))
    many(nx - half, 2, lambda x: finish(x + half, x + 2, 1))


def lane_padded(size):
    return -(-size // LANES) * LANES


def banded_table(channels, ny, rows):
    table = np.zeros((channels, 3, 3, 3, ny + 2, 3, 3, channels, rows), np.float32)
    for c in range(channels):
        for x in range(3):
            for d in range(3):
                for z in range(3):
                    for p in range(ny + 2):
                        table[c, x, d, z, p, x, z, c, p + d + 1] = 1.0
    table = table.reshape(27 * channels, ny + 2, 9 * channels * rows)
    extra = lane_padded(table.shape[2]) - table.shape[2]
    return np.pad(table, ((0, 0), (0, 0), (0, extra)))


def returned_table(channels, ny):
    table = np.zeros((channels, 3, 3, 3, ny + 2, 3, 3, channels, ny), np.float32)
    for c in range(channels):
        for x in range(3):
            for d in range(3):
                for z in range(3):
                    for y in range(ny):
                        table[c, x, d, z, y + 2 - d, x, z, c, y] = 1.0
    table = table.reshape(27 * channels, ny + 2, 9 * channels * ny)
    extra = lane_padded(table.shape[2]) - table.shape[2]
    return np.pad(table, ((0, 0), (0, 0), (0, extra)))


def spread(weight, table):
    flat = table.reshape(table.shape[0], -1)
    wide = jnp.dot(
        weight, jnp.asarray(flat, jnp.bfloat16), preferred_element_type=jnp.float32
    ).astype(jnp.bfloat16)
    columns = table.shape[2]
    return jnp.concatenate(
        [wide[:, p * columns : (p + 1) * columns] for p in range(table.shape[1])], axis=0
    )


def input_weights(weight_in, bias_in, ny, rows):
    hid, comp = weight_in.shape[:2]
    w1 = spread(weight_in.reshape(hid, -1), banded_table(comp, ny, rows))
    return w1, jnp.tile(bias_in, ny + 2)[:, None]


def output_weights(weight_in, weight_out, ny, rows):
    hid, comp = weight_in.shape[:2]
    flipped = jnp.flip(weight_out, (2, 3, 4)).transpose(1, 0, 2, 3, 4).reshape(hid, -1)
    w2 = spread(flipped, banded_table(weight_out.shape[0], ny, rows))
    w3 = spread(weight_in.reshape(hid, -1), returned_table(comp, ny)).T[: 9 * comp * ny]
    return w2, w3


def velocity_step(vel_ext, w1, bias, nx, ny, spacings):
    rows = vel_ext.shape[2]
    half = (nx + 2) // 2
    vm = pl.BlockSpec(memory_space=pltpu.VMEM)
    return pl.pallas_call(
        functools.partial(velocity_kernel, (nx, ny, rows, half, spacings)),
        out_shape=(
            jax.ShapeDtypeStruct((half * w1.shape[0], 2 * LANES), jnp.bfloat16),
            jax.ShapeDtypeStruct((9, nx, ny, LANES), jnp.float32),
        ),
        in_specs=[vm] * 3,
        out_specs=(vm, vm),
        scratch_shapes=[pltpu.VMEM(((half + 2) * 9 * rows, 2 * LANES), jnp.bfloat16)],
        compiler_params=pltpu.CompilerParams(vmem_limit_bytes=40 * 2**20),
        cost_estimate=pl.CostEstimate(
            flops=2 * half * w1.shape[0] * w1.shape[1] * 2 * LANES,
            bytes_accessed=12 * 2**20,
            transcendentals=half * w1.shape[0] * 2 * LANES,
        ),
        name="velocity",
    )(vel_ext, w1, bias)


def closure_step(vel_ext, lam_ext, slope, grads, w2, w3, nx, ny, spacings):
    rows = vel_ext.shape[2]
    half = (nx + 2) // 2
    vm = pl.BlockSpec(memory_space=pltpu.VMEM)
    return pl.pallas_call(
        functools.partial(closure_kernel, (nx, ny, rows, half, spacings)),
        out_shape=jax.ShapeDtypeStruct((3, nx, ny, LANES), jnp.float32),
        in_specs=[vm] * 6,
        out_specs=vm,
        scratch_shapes=[
            pltpu.VMEM(((half + 2) * 18 * rows, 2 * LANES), jnp.bfloat16),
            pltpu.VMEM((half + 2, 9 * ny, 2 * LANES), jnp.float32),
        ],
        compiler_params=pltpu.CompilerParams(vmem_limit_bytes=50 * 2**20),
        name="closure",
    )(vel_ext, lam_ext, slope, grads, w2, w3)


def waves(length, modes):
    products = np.arange(length)[:, None] * np.arange(modes)[None, :] % length
    phases = products.astype(np.float64) * (2.0 * math.pi / length)
    return np.cos(phases), np.sin(phases)


def f32(table):
    return jnp.asarray(np.asarray(table, np.float32))


def project(re, im, index_x, index_y, index_z, sizes):
    NX, NY, NZ = sizes

    def signed(index, length):
        return jnp.where(index > length // 2, index - length, index).astype(jnp.float32)

    wx, wy, wz = signed(index_x, NX), signed(index_y, NY), signed(index_z, NZ)
    squared = wx * wx + wy * wy + wz * wz
    keep = (index_x != NX // 2) & (index_y != NY // 2) & (index_z != NZ // 2)
    inverse = jnp.where(squared > 0, 1.0 / jnp.maximum(squared, 1.0), 0.0)
    done = []
    for part in (re, im):
        dotted = (wx * part[0] + wy * part[1] + wz * part[2]) * inverse
        done.append([jnp.where(keep, part[c] - w * dotted, 0.0) for c, w in enumerate((wx, wy, wz))])
    return jnp.stack(done[0]), jnp.stack(done[1])


def einsum(*args):
    return jnp.einsum(*args, precision=high)


def mode_weights(NX, NY, NZ):
    scale = np.full((NZ // 2,), 2.0 / (NX * NY * NZ))
    scale[0] /= 2.0
    return scale


def halves(table):
    table = np.asarray(table, np.float32)
    first = table.astype(ml_dtypes.bfloat16)
    second = (table - first.astype(np.float32)).astype(ml_dtypes.bfloat16)
    return jnp.asarray(np.stack([first, second]))


def cut(value):
    first = value.astype(jnp.bfloat16)
    return first, (value - first.astype(jnp.float32)).astype(jnp.bfloat16)


def dot3(left, right, dims=((1,), (0,))):
    def one(a, b):
        return lax.dot_general(a, b, (dims, ((), ())), preferred_element_type=jnp.float32)

    return one(left[0], right[0]) + (one(left[0], right[1]) + one(left[1], right[0]))


def forward_kernel(sizes, cot, table, sent):
    total, nj, nx, ny = sizes
    left = (table[0], table[1])
    for c in range(3):
        planes = []
        for y in range(ny):
            modes = dot3(left, cut(cot[c, :, y, :]), ((1,), (1,)))
            rows = 2 * total
            planes.append(
                jnp.concatenate([modes[j * rows : (j + 1) * rows] for j in range(nj)], axis=1)
            )
        block = jnp.swapaxes(jnp.stack(planes), 0, 1)
        sent[:, :, c] = block.reshape(total, 2, ny, nj * nx)


def backward_kernel(sizes, got, table, lam):
    total, nj, nx, ny = sizes
    right = (table[0], table[1])
    for c in range(3):
        block = got[:, :, c].reshape(2 * total, ny, nj * nx)
        block = jnp.swapaxes(block, 0, 1)
        for y in range(ny):
            modes = jnp.concatenate(
                [block[y][:, j * nx : (j + 1) * nx] for j in range(nj)], axis=0
            )
            lam[c, :, y, :] = dot3(cut(modes), right, ((0,), (0,)))


def middle_kernel(sizes, got, lanes, fy, fx, bx, by, sent):
    npx, npy, ny, NY, wide = sizes
    rows = 2 * npy * ny
    per = wide // npx

    def table(ref):
        return ref[0], ref[1]

    modes = []
    for c in range(3):
        block = jnp.concatenate(
            [got[h * npy : (h + 1) * npy, :, c].reshape(rows, per) for h in range(npx)], axis=1
        )
        mixed = dot3(table(fy), cut(block))
        both = dot3(cut(mixed), table(fx))
        re = both[:NY, :wide] + both[NY:, wide:]
        im = both[NY:, :wide] - both[:NY, wide:]
        modes.append((re, im))
    ky = lax.broadcasted_iota(jnp.int32, (NY, wide), 0)
    wy = jnp.where(ky > NY // 2, ky - NY, ky).astype(jnp.float32)
    wx, wz = lanes[0:1], lanes[1:2]
    keep = jnp.where(ky == NY // 2, 0.0, 1.0) * lanes[2:3]
    squared = wx * wx + wy * wy + wz * wz
    inverse = jnp.where(squared > 0, 1.0 / jnp.maximum(squared, 1.0), 0.0)
    dotted = [
        (wx * modes[0][r] + wy * modes[1][r] + wz * modes[2][r]) * inverse for r in range(2)
    ]
    for c, w in enumerate((wx, wy, wz)):
        pair = jnp.concatenate([(modes[c][r] - w * dotted[r]) * keep for r in range(2)], axis=0)
        both = dot3(cut(pair), table(bx))
        re = both[:NY, :wide] - both[NY:, wide:]
        im = both[NY:, :wide] + both[:NY, wide:]
        back = dot3(table(by), cut(jnp.concatenate([re, im], axis=0)))
        for h in range(npx):
            sent[h * npy : (h + 1) * npy, :, c] = back[:, h * per : (h + 1) * per].reshape(
                npy, 2, ny, per
            )


def local_call(kernel, shape, name, *operands):
    vm = pl.BlockSpec(memory_space=pltpu.VMEM)
    return pl.pallas_call(
        kernel,
        out_shape=jax.ShapeDtypeStruct(shape, jnp.float32),
        in_specs=[vm] * len(operands),
        out_specs=vm,
        compiler_params=pltpu.CompilerParams(vmem_limit_bytes=40 * 2**20),
        name=name,
    )(*operands)


def projected_once(cotangent, sizes, npx, npy, others, beside_first, beside_second):
    NX, NY, NZ = sizes
    _, nx, ny, _ = cotangent.shape
    total = npx * npy
    nj = NZ // 2 // total
    cz, sz = waves(NZ, NZ // 2)
    cy, sy = waves(NY, NY)
    cx, sx = waves(NX, NX)
    shape = (total, 2, 3, ny, nj * nx)
    forward_z = np.stack([cz, -sz], 0).reshape(2, NZ, total, nj)
    forward_z = forward_z.transpose(3, 2, 0, 1).reshape(NZ, NZ)
    sent = local_call(
        functools.partial(forward_kernel, (total, nj, nx, ny)),
        shape,
        "forward",
        cotangent,
        halves(forward_z),
    )
    sent, others = lax.optimization_barrier((sent, others))
    got = lax.all_to_all(sent, ("px", "py"), 0, 0, tiled=True)
    first, halo_first = beside_first(*others)
    got, first = lax.optimization_barrier((got, first))
    forward_y = np.stack([np.stack([cy, -sy], 0), np.stack([sy, cy], 0)], 0)
    forward_y = forward_y.reshape(2, 2, npy, ny, NY).transpose(1, 4, 2, 0, 3)
    eye = np.eye(nj)
    forward_x = np.stack([cx, sx], 0).reshape(2, npx, nx, NX)
    forward_x = np.einsum("shxm,jk->hjxskm", forward_x, eye)
    backward_x = np.stack([cx, sx], 0).reshape(2, NX, npx, nx)
    backward_x = np.einsum("smhx,jk->jmshkx", backward_x, eye)
    backward_y = np.stack([np.stack([cy, sy], 0), np.stack([-sy, cy], 0)], 0)
    backward_y = backward_y.reshape(2, 2, NY, npy, ny).transpose(3, 1, 4, 0, 2)
    wide = nj * NX
    me = lax.axis_index("px") * npy + lax.axis_index("py")
    lane = jnp.arange(wide, dtype=jnp.int32)
    index_x, index_z = lane % NX, me * nj + lane // NX
    wave_x = jnp.where(index_x > NX // 2, index_x - NX, index_x).astype(jnp.float32)
    keep = ((index_x != NX // 2) & (index_z != NZ // 2)).astype(jnp.float32)
    lanes = jnp.stack([wave_x, index_z.astype(jnp.float32), keep])
    sent = local_call(
        functools.partial(middle_kernel, (npx, npy, ny, NY, wide)),
        shape,
        "middle",
        got,
        lanes,
        halves(forward_y.reshape(2 * NY, 2 * NY)),
        halves(forward_x.reshape(wide, 2 * wide)),
        halves(backward_x.reshape(wide, 2 * wide)),
        halves(backward_y.reshape(2 * NY, 2 * NY)),
    )
    sent, first, halo_first = lax.optimization_barrier((sent, first, halo_first))
    got = lax.all_to_all(sent, ("px", "py"), 0, 0, tiled=True)
    got, second = lax.optimization_barrier((got, beside_second(first, halo_first)))
    scale = mode_weights(NX, NY, NZ)
    backward_z = np.stack([(cz * scale).T, (-sz * scale).T], 0).reshape(2, total, nj, NZ)
    backward_z = backward_z.transpose(2, 1, 0, 3).reshape(NZ, NZ)
    lam = local_call(
        functools.partial(backward_kernel, (total, nj, nx, ny)),
        cotangent.shape,
        "backward",
        got,
        halves(backward_z),
    )
    return lam, second


def projected_twice(cotangent, sizes, npx, npy):
    NX, NY, NZ = sizes
    cz, sz = waves(NZ, NZ // 2)
    cy, sy = map(f32, waves(NY, NY))
    cx, sx = map(f32, waves(NX, NX))
    scale = mode_weights(NX, NY, NZ)
    stacked = jnp.stack(
        [einsum("cxyz,zk->cxyk", cotangent, f32(cz)), einsum("cxyz,zk->cxyk", cotangent, f32(-sz))]
    )
    re, im = lax.all_to_all(stacked, "py", split_axis=4, concat_axis=3, tiled=True)
    pair = jnp.stack(
        [
            einsum("cxyk,yl->ckxl", re, cy) + einsum("cxyk,yl->ckxl", im, sy),
            einsum("cxyk,yl->ckxl", im, cy) - einsum("cxyk,yl->ckxl", re, sy),
        ]
    )
    re, im = lax.all_to_all(pair, "px", split_axis=4, concat_axis=3, tiled=True)
    re, im = (
        einsum("ckxl,xm->cklm", re, cx) + einsum("ckxl,xm->cklm", im, sx),
        einsum("ckxl,xm->cklm", im, cx) - einsum("ckxl,xm->cklm", re, sx),
    )
    nk, nl = re.shape[1], re.shape[2]
    index_z = (lax.axis_index("py") * nk + jnp.arange(nk, dtype=jnp.int32))[:, None, None]
    index_y = (lax.axis_index("px") * nl + jnp.arange(nl, dtype=jnp.int32))[None, :, None]
    index_x = jnp.arange(NX, dtype=jnp.int32)[None, None, :]
    re, im = project(re, im, index_x, index_y, index_z, sizes)
    pair = jnp.stack(
        [
            einsum("cklm,mx->ckxl", re, cx) - einsum("cklm,mx->ckxl", im, sx),
            einsum("cklm,mx->ckxl", re, sx) + einsum("cklm,mx->ckxl", im, cx),
        ]
    )
    re, im = lax.all_to_all(pair, "px", split_axis=3, concat_axis=4, tiled=True)
    pair = jnp.stack(
        [
            einsum("ckxl,ly->cxyk", re, cy) - einsum("ckxl,ly->cxyk", im, sy),
            einsum("ckxl,ly->cxyk", re, sy) + einsum("ckxl,ly->cxyk", im, cy),
        ]
    )
    re, im = lax.all_to_all(pair, "py", split_axis=3, concat_axis=4, tiled=True)
    return einsum("cxyk,kz->cxyz", re, f32((cz * scale).T)) - einsum(
        "cxyk,kz->cxyz", im, f32((sz * scale).T)
    )


def body(velocity, cotangent, weight_in, bias_in, weight_out):
    npx, npy = lax.axis_size("px"), lax.axis_size("py")
    _, nx, ny, NZ = velocity.shape
    sizes = (nx * npx, ny * npy, NZ)
    spacings = tuple(2.0 * math.pi / size for size in sizes)
    rows = rows_of(ny)

    def beside_first(velocity, weight_in, bias_in, weight_out):
        w1, bias = input_weights(weight_in, bias_in, ny, rows)
        w2, w3 = output_weights(weight_in, weight_out, ny, rows)
        return (w1, bias, w2, w3), (velocity,) + halo(velocity, "py", 2, 3)

    def beside_second(first, halo_first):
        w1, bias, w2, w3 = first
        vel_ext = bordered_rest(*halo_first)
        slope, grads = velocity_step(vel_ext, w1, bias, nx, ny, spacings)
        return vel_ext, slope, grads, w2, w3

    others = (velocity, weight_in, bias_in, weight_out)
    if (NZ // 2) % (npx * npy) == 0 and nx * (NZ // 2) % (npx * npy * LANES) == 0 and ny % 8 == 0:
        lam, second = projected_once(cotangent, sizes, npx, npy, others, beside_first, beside_second)
    else:
        lam = projected_twice(cotangent, sizes, npx, npy)
        second = beside_second(*beside_first(*others))
    vel_ext, slope, grads, w2, w3 = second
    return closure_step(vel_ext, bordered(lam), slope, grads, w2, w3, nx, ny, spacings)


def solution(mesh):
    placed = (P(None, "px", "py", None), P(None, "px", "py", None), P(), P(), P())
    return jax.shard_map(
        body, mesh=mesh, in_specs=placed, out_specs=P(None, "px", "py", None), check_vma=False
    )
```

```python
import functools
import math

import jax
import jax.numpy as jnp
import ml_dtypes
import numpy as np
from jax import lax
from jax.experimental import pallas as pl
from jax.experimental.pallas import tpu as pltpu
from jax.sharding import PartitionSpec as P

time_step = 0.005
high = lax.Precision.HIGH
LANES = 128
taps = ((1, 45.0), (2, -9.0), (3, 1.0))


def rows_of(ny):
    return -(-(ny + 6) // 8) * 8


def halo(block, axis, dim, width):
    count = lax.axis_size(axis)
    forward = [(i, (i + 1) % count) for i in range(count)]
    backward = [(target, source) for source, target in forward]
    low = lax.ppermute(
        lax.slice_in_dim(block, block.shape[dim] - width, None, axis=dim), axis, forward
    )
    high_side = lax.ppermute(lax.slice_in_dim(block, 0, width, axis=dim), axis, backward)
    return low, high_side


def widened(block, low, up):
    ny = block.shape[2]
    extra = rows_of(ny) - ny - 6
    parts = [block, up]
    if extra:
        parts.append(jnp.zeros(block.shape[:2] + (extra,) + block.shape[3:], block.dtype))
    return jnp.concatenate(parts + [low], axis=2)


def bordered(block):
    wide = widened(block, *halo(block, "py", 2, 3))
    low, up = halo(wide, "px", 1, 3)
    return jnp.concatenate([low, wide, up], axis=1)


def zroll(value, shift):
    return pltpu.roll(value, shift % LANES, value.ndim - 1)


def many(count, size, run):
    if count % size:
        size = 1

    @pl.loop(0, count // size)
    def _(block):
        for piece in range(size):
            run(block * size + piece)


def velocity_kernel(sizes, vel, w1, b1, slope, grads, vs):
    nx, ny, rows, half, spacings = sizes
    vblock, out_rows = 9 * rows, w1.shape[0]

    def prepare(k):
        for side in range(2):
            v = vel[:, k + 1 + side * half].reshape(3 * rows, LANES)
            for t in range(3):
                start = pl.multiple_of(k * vblock + t * 3 * rows, 16)
                vs[pl.ds(start, 3 * rows), side * LANES : (side + 1) * LANES] = zroll(
                    v, 1 - t
                ).astype(jnp.bfloat16)

    many(half + 2, 5, prepare)

    def step(i):
        pre = jnp.dot(
            w1[:, : 3 * vblock],
            vs[pl.ds(pl.multiple_of(i * vblock, 16), 3 * vblock), :],
            preferred_element_type=jnp.float32,
        )
        t = jnp.tanh(pre + b1[...])
        slope[pl.ds(pl.multiple_of(i * out_rows, 16), out_rows), :] = (1.0 - t * t).astype(
            jnp.bfloat16
        )

    many(half, 3, step)

    def gradient(x):
        e = x + 3
        for c in range(3):
            wide = vel[c, e]
            for b in range(3):
                total = 0.0
                for d, weight in taps:
                    if b == 0:
                        pair = vel[c, e + d, :ny] - vel[c, e - d, :ny]
                    elif b == 1:
                        pair = (pltpu.roll(wide, rows - d, 0) - pltpu.roll(wide, d, 0))[:ny]
                    else:
                        pair = zroll(wide[:ny], -d) - zroll(wide[:ny], d)
                    total += (weight / (60.0 * spacings[b])) * pair
                grads[3 * b + c, x] = total

    many(nx, 2, gradient)


def closure_kernel(sizes, vel, lam, slope, grads, w2, w3, out, ss, acc):
    nx, ny, rows, half, spacings = sizes
    sblock, hid_rows = 18 * rows, w2.shape[0]
    inv2 = [1.0 / (2.0 * h) for h in spacings]

    def prepare(k):
        for side in range(2):
            e = k + 1 + side * half
            lanes = slice(side * LANES, (side + 1) * LANES)
            l = [lam[c, e] for c in range(3)]
            dx = [(lam[c, e + 1] - lam[c, e - 1]) * inv2[0] for c in range(3)]
            dy = [
                (pltpu.roll(l[c], rows - 1, 0) - pltpu.roll(l[c], 1, 0)) * inv2[1]
                for c in range(3)
            ]
            dz = [(zroll(l[c], -1) - zroll(l[c], 1)) * inv2[2] for c in range(3)]
            s = jnp.concatenate(
                [dx[0], dy[1], dz[2], dy[0] + dx[1], dz[0] + dx[2], dz[1] + dy[2]], axis=0
            )
            for t in range(3):
                start = pl.multiple_of(k * sblock + t * 6 * rows, 16)
                ss[pl.ds(start, 6 * rows), lanes] = zroll(s, 1 - t).astype(jnp.bfloat16)
        acc[k] = jnp.zeros(acc.shape[1:], acc.dtype)

    many(half + 2, 5, prepare)

    def step(i):
        hid = jnp.dot(
            w2[:, : 3 * sblock],
            ss[pl.ds(pl.multiple_of(i * sblock, 16), 3 * sblock), :],
            preferred_element_type=jnp.float32,
        )
        part = slope[pl.ds(pl.multiple_of(i * hid_rows, 16), hid_rows), :]
        p = (hid * part.astype(jnp.float32)).astype(jnp.bfloat16)
        c = jnp.dot(w3[...], p, preferred_element_type=jnp.float32)
        for d in range(3):
            acc[i + d] += c[d * 9 * ny : (d + 1) * 9 * ny]

    many(half, 3, step)

    for d in range(2):
        acc[half + d, :, :LANES] += acc[d, :, LANES:]

    def finish(x, idx, side):
        e = x + 3
        lanes = slice(side * LANES, (side + 1) * LANES)
        low = [acc[idx, d * 3 * ny : (d + 1) * 3 * ny, lanes] for d in range(3)]
        closure = zroll(low[0], -1) + low[1] + zroll(low[2], 1)
        wide = [lam[c, e] for c in range(3)]
        l0 = [value[:ny] for value in wide]
        vy = vel[1, e]
        vz = vel[2, e, :ny]
        vx = {q: vel[0, e + q, :ny] for d, _ in taps for q in (d, -d)}
        for c in range(3):
            total = closure[c * ny : (c + 1) * ny]
            ly = wide[c] * vy
            lz = l0[c] * vz
            for d, weight in taps:
                fx = lam[c, e + d, :ny] * vx[d] - lam[c, e - d, :ny] * vx[-d]
                fy = (pltpu.roll(ly, rows - d, 0) - pltpu.roll(ly, d, 0))[:ny]
                fz = zroll(lz, -d) - zroll(lz, d)
                for b, pair in enumerate((fx, fy, fz)):
                    total += (weight / (60.0 * spacings[b])) * pair
            for a in range(3):
                total -= l0[a] * grads[3 * c + a, x]
            out[c, x] = l0[c] + time_step * total

    many(half, 3, lambda x: finish(x, x + 2, 0))
    many(nx - half, 2, lambda x: finish(x + half, x + 2, 1))


def lane_padded(size):
    return -(-size // LANES) * LANES


def banded_table(channels, ny, rows):
    table = np.zeros((channels, 3, 3, 3, ny + 2, 3, 3, channels, rows), np.float32)
    for c in range(channels):
        for x in range(3):
            for d in range(3):
                for z in range(3):
                    for p in range(ny + 2):
                        table[c, x, d, z, p, x, z, c, (p + d - 2) % rows] = 1.0
    table = table.reshape(27 * channels, ny + 2, 9 * channels * rows)
    extra = lane_padded(table.shape[2]) - table.shape[2]
    return np.pad(table, ((0, 0), (0, 0), (0, extra)))


def returned_table(channels, ny):
    table = np.zeros((channels, 3, 3, 3, ny + 2, 3, 3, channels, ny), np.float32)
    for c in range(channels):
        for x in range(3):
            for d in range(3):
                for z in range(3):
                    for y in range(ny):
                        table[c, x, d, z, y + 2 - d, x, z, c, y] = 1.0
    table = table.reshape(27 * channels, ny + 2, 9 * channels * ny)
    extra = lane_padded(table.shape[2]) - table.shape[2]
    return np.pad(table, ((0, 0), (0, 0), (0, extra)))


def spread(weight, table):
    flat = table.reshape(table.shape[0], -1)
    wide = jnp.dot(
        weight, jnp.asarray(flat, jnp.bfloat16), preferred_element_type=jnp.float32
    ).astype(jnp.bfloat16)
    columns = table.shape[2]
    return jnp.concatenate(
        [wide[:, p * columns : (p + 1) * columns] for p in range(table.shape[1])], axis=0
    )


def input_weights(weight_in, bias_in, ny, rows):
    hid, comp = weight_in.shape[:2]
    w1 = spread(weight_in.reshape(hid, -1), banded_table(comp, ny, rows))
    return w1, jnp.tile(bias_in, ny + 2)[:, None]


def output_weights(weight_in, weight_out, ny, rows):
    hid, comp = weight_in.shape[:2]
    flipped = jnp.flip(weight_out, (2, 3, 4)).transpose(1, 0, 2, 3, 4).reshape(hid, -1)
    w2 = spread(flipped, banded_table(weight_out.shape[0], ny, rows))
    w3 = spread(weight_in.reshape(hid, -1), returned_table(comp, ny)).T[: 9 * comp * ny]
    return w2, w3


def velocity_step(vel_ext, w1, bias, nx, ny, spacings):
    rows = vel_ext.shape[2]
    half = (nx + 2) // 2
    vm = pl.BlockSpec(memory_space=pltpu.VMEM)
    return pl.pallas_call(
        functools.partial(velocity_kernel, (nx, ny, rows, half, spacings)),
        out_shape=(
            jax.ShapeDtypeStruct((half * w1.shape[0], 2 * LANES), jnp.bfloat16),
            jax.ShapeDtypeStruct((9, nx, ny, LANES), jnp.float32),
        ),
        in_specs=[vm] * 3,
        out_specs=(vm, vm),
        scratch_shapes=[pltpu.VMEM(((half + 2) * 9 * rows, 2 * LANES), jnp.bfloat16)],
        compiler_params=pltpu.CompilerParams(vmem_limit_bytes=20 * 2**20),
        cost_estimate=pl.CostEstimate(
            flops=2 * half * w1.shape[0] * w1.shape[1] * 2 * LANES,
            bytes_accessed=12 * 2**20,
            transcendentals=half * w1.shape[0] * 2 * LANES,
        ),
        name="velocity",
    )(vel_ext, w1, bias)


def closure_step(vel_ext, lam_ext, slope, grads, w2, w3, nx, ny, spacings):
    rows = vel_ext.shape[2]
    half = (nx + 2) // 2
    vm = pl.BlockSpec(memory_space=pltpu.VMEM)
    return pl.pallas_call(
        functools.partial(closure_kernel, (nx, ny, rows, half, spacings)),
        out_shape=jax.ShapeDtypeStruct((3, nx, ny, LANES), jnp.float32),
        in_specs=[vm] * 6,
        out_specs=vm,
        scratch_shapes=[
            pltpu.VMEM(((half + 2) * 18 * rows, 2 * LANES), jnp.bfloat16),
            pltpu.VMEM((half + 2, 9 * ny, 2 * LANES), jnp.float32),
        ],
        compiler_params=pltpu.CompilerParams(vmem_limit_bytes=28 * 2**20),
        name="closure",
    )(vel_ext, lam_ext, slope, grads, w2, w3)


def waves(length, modes):
    products = np.arange(length)[:, None] * np.arange(modes)[None, :] % length
    phases = products.astype(np.float64) * (2.0 * math.pi / length)
    return np.cos(phases), np.sin(phases)


def f32(table):
    return jnp.asarray(np.asarray(table, np.float32))


def project(re, im, index_x, index_y, index_z, sizes):
    NX, NY, NZ = sizes

    def signed(index, length):
        return jnp.where(index > length // 2, index - length, index).astype(jnp.float32)

    wx, wy, wz = signed(index_x, NX), signed(index_y, NY), signed(index_z, NZ)
    squared = wx * wx + wy * wy + wz * wz
    keep = (index_x != NX // 2) & (index_y != NY // 2) & (index_z != NZ // 2)
    inverse = jnp.where(squared > 0, 1.0 / jnp.maximum(squared, 1.0), 0.0)
    done = []
    for part in (re, im):
        dotted = (wx * part[0] + wy * part[1] + wz * part[2]) * inverse
        done.append([jnp.where(keep, part[c] - w * dotted, 0.0) for c, w in enumerate((wx, wy, wz))])
    return jnp.stack(done[0]), jnp.stack(done[1])


def einsum(*args):
    return jnp.einsum(*args, precision=high)


def mode_weights(NX, NY, NZ):
    scale = np.full((NZ // 2,), 2.0 / (NX * NY * NZ))
    scale[0] /= 2.0
    return scale


def halves(table):
    table = np.asarray(table, np.float32)
    first = table.astype(ml_dtypes.bfloat16)
    second = (table - first.astype(np.float32)).astype(ml_dtypes.bfloat16)
    return jnp.asarray(np.stack([first, second]))


def cut(value):
    first = value.astype(jnp.bfloat16)
    return first, (value - first.astype(jnp.float32)).astype(jnp.bfloat16)


def dot3(left, right, dims=((1,), (0,))):
    def one(a, b):
        return lax.dot_general(a, b, (dims, ((), ())), preferred_element_type=jnp.float32)

    return one(left[0], right[0]) + (one(left[0], right[1]) + one(left[1], right[0]))


def forward_kernel(sizes, cot, table, sent):
    total, nj, nx, ny = sizes
    left = (table[0], table[1])
    for c in range(3):
        planes = []
        for y in range(ny):
            modes = dot3(left, cut(cot[c, :, y, :]), ((1,), (1,)))
            rows = 2 * total
            planes.append(
                jnp.concatenate([modes[j * rows : (j + 1) * rows] for j in range(nj)], axis=1)
            )
        block = jnp.swapaxes(jnp.stack(planes), 0, 1)
        sent[:, :, c] = block.reshape(total, 2, ny, nj * nx)


def backward_kernel(sizes, got, table, lam):
    total, nj, nx, ny = sizes
    right = (table[0], table[1])
    for c in range(3):
        block = got[:, :, c].reshape(2 * total, ny, nj * nx)
        block = jnp.swapaxes(block, 0, 1)
        for y in range(ny):
            modes = jnp.concatenate(
                [block[y][:, j * nx : (j + 1) * nx] for j in range(nj)], axis=0
            )
            lam[c, :, y, :] = dot3(cut(modes), right, ((0,), (0,)))


def middle_kernel(sizes, got, lanes, fy, fx, bx, by, sent):
    npx, npy, ny, NY, wide = sizes
    rows = 2 * npy * ny
    per = wide // npx

    def table(ref):
        return ref[0], ref[1]

    modes = []
    for c in range(3):
        block = jnp.concatenate(
            [got[h * npy : (h + 1) * npy, :, c].reshape(rows, per) for h in range(npx)], axis=1
        )
        mixed = dot3(table(fy), cut(block))
        both = dot3(cut(mixed), table(fx))
        re = both[:NY, :wide] + both[NY:, wide:]
        im = both[NY:, :wide] - both[:NY, wide:]
        modes.append((re, im))
    ky = lax.broadcasted_iota(jnp.int32, (NY, wide), 0)
    wy = jnp.where(ky > NY // 2, ky - NY, ky).astype(jnp.float32)
    wx, wz = lanes[0:1], lanes[1:2]
    keep = jnp.where(ky == NY // 2, 0.0, 1.0) * lanes[2:3]
    squared = wx * wx + wy * wy + wz * wz
    inverse = jnp.where(squared > 0, 1.0 / jnp.maximum(squared, 1.0), 0.0)
    dotted = [
        (wx * modes[0][r] + wy * modes[1][r] + wz * modes[2][r]) * inverse for r in range(2)
    ]
    for c, w in enumerate((wx, wy, wz)):
        pair = jnp.concatenate([(modes[c][r] - w * dotted[r]) * keep for r in range(2)], axis=0)
        both = dot3(cut(pair), table(bx))
        re = both[:NY, :wide] - both[NY:, wide:]
        im = both[NY:, :wide] + both[:NY, wide:]
        back = dot3(table(by), cut(jnp.concatenate([re, im], axis=0)))
        for h in range(npx):
            sent[h * npy : (h + 1) * npy, :, c] = back[:, h * per : (h + 1) * per].reshape(
                npy, 2, ny, per
            )


def local_call(kernel, shape, name, *operands):
    vm = pl.BlockSpec(memory_space=pltpu.VMEM)
    return pl.pallas_call(
        kernel,
        out_shape=jax.ShapeDtypeStruct(shape, jnp.float32),
        in_specs=[vm] * len(operands),
        out_specs=vm,
        compiler_params=pltpu.CompilerParams(vmem_limit_bytes=40 * 2**20),
        name=name,
    )(*operands)


def projected_once(cotangent, sizes, npx, npy, others, beside_first, beside_second):
    NX, NY, NZ = sizes
    _, nx, ny, _ = cotangent.shape
    total = npx * npy
    nj = NZ // 2 // total
    cz, sz = waves(NZ, NZ // 2)
    cy, sy = waves(NY, NY)
    cx, sx = waves(NX, NX)
    shape = (total, 2, 3, ny, nj * nx)
    forward_z = np.stack([cz, -sz], 0).reshape(2, NZ, total, nj)
    forward_z = forward_z.transpose(3, 2, 0, 1).reshape(NZ, NZ)
    sent = local_call(
        functools.partial(forward_kernel, (total, nj, nx, ny)),
        shape,
        "forward",
        cotangent,
        halves(forward_z),
    )
    sent, others = lax.optimization_barrier((sent, others))
    got = lax.all_to_all(sent, ("px", "py"), 0, 0, tiled=True)
    first, halo_first = beside_first(*others)
    got, first = lax.optimization_barrier((got, first))
    forward_y = np.stack([np.stack([cy, -sy], 0), np.stack([sy, cy], 0)], 0)
    forward_y = forward_y.reshape(2, 2, npy, ny, NY).transpose(1, 4, 2, 0, 3)
    eye = np.eye(nj)
    forward_x = np.stack([cx, sx], 0).reshape(2, npx, nx, NX)
    forward_x = np.einsum("shxm,jk->hjxskm", forward_x, eye)
    backward_x = np.stack([cx, sx], 0).reshape(2, NX, npx, nx)
    backward_x = np.einsum("smhx,jk->jmshkx", backward_x, eye)
    backward_y = np.stack([np.stack([cy, sy], 0), np.stack([-sy, cy], 0)], 0)
    backward_y = backward_y.reshape(2, 2, NY, npy, ny).transpose(3, 1, 4, 0, 2)
    wide = nj * NX
    me = lax.axis_index("px") * npy + lax.axis_index("py")
    lane = jnp.arange(wide, dtype=jnp.int32)
    index_x, index_z = lane % NX, me * nj + lane // NX
    wave_x = jnp.where(index_x > NX // 2, index_x - NX, index_x).astype(jnp.float32)
    keep = ((index_x != NX // 2) & (index_z != NZ // 2)).astype(jnp.float32)
    lanes = jnp.stack([wave_x, index_z.astype(jnp.float32), keep])
    sent = local_call(
        functools.partial(middle_kernel, (npx, npy, ny, NY, wide)),
        shape,
        "middle",
        got,
        lanes,
        halves(forward_y.reshape(2 * NY, 2 * NY)),
        halves(forward_x.reshape(wide, 2 * wide)),
        halves(backward_x.reshape(wide, 2 * wide)),
        halves(backward_y.reshape(2 * NY, 2 * NY)),
    )
    sent, first, halo_first = lax.optimization_barrier((sent, first, halo_first))
    got = lax.all_to_all(sent, ("px", "py"), 0, 0, tiled=True)
    got, second = lax.optimization_barrier((got, beside_second(first, halo_first)))
    scale = mode_weights(NX, NY, NZ)
    backward_z = np.stack([(cz * scale).T, (-sz * scale).T], 0).reshape(2, total, nj, NZ)
    backward_z = backward_z.transpose(2, 1, 0, 3).reshape(NZ, NZ)
    lam = local_call(
        functools.partial(backward_kernel, (total, nj, nx, ny)),
        cotangent.shape,
        "backward",
        got,
        halves(backward_z),
    )
    return lam, second


def projected_twice(cotangent, sizes, npx, npy):
    NX, NY, NZ = sizes
    cz, sz = waves(NZ, NZ // 2)
    cy, sy = map(f32, waves(NY, NY))
    cx, sx = map(f32, waves(NX, NX))
    scale = mode_weights(NX, NY, NZ)
    stacked = jnp.stack(
        [einsum("cxyz,zk->cxyk", cotangent, f32(cz)), einsum("cxyz,zk->cxyk", cotangent, f32(-sz))]
    )
    re, im = lax.all_to_all(stacked, "py", split_axis=4, concat_axis=3, tiled=True)
    pair = jnp.stack(
        [
            einsum("cxyk,yl->ckxl", re, cy) + einsum("cxyk,yl->ckxl", im, sy),
            einsum("cxyk,yl->ckxl", im, cy) - einsum("cxyk,yl->ckxl", re, sy),
        ]
    )
    re, im = lax.all_to_all(pair, "px", split_axis=4, concat_axis=3, tiled=True)
    re, im = (
        einsum("ckxl,xm->cklm", re, cx) + einsum("ckxl,xm->cklm", im, sx),
        einsum("ckxl,xm->cklm", im, cx) - einsum("ckxl,xm->cklm", re, sx),
    )
    nk, nl = re.shape[1], re.shape[2]
    index_z = (lax.axis_index("py") * nk + jnp.arange(nk, dtype=jnp.int32))[:, None, None]
    index_y = (lax.axis_index("px") * nl + jnp.arange(nl, dtype=jnp.int32))[None, :, None]
    index_x = jnp.arange(NX, dtype=jnp.int32)[None, None, :]
    re, im = project(re, im, index_x, index_y, index_z, sizes)
    pair = jnp.stack(
        [
            einsum("cklm,mx->ckxl", re, cx) - einsum("cklm,mx->ckxl", im, sx),
            einsum("cklm,mx->ckxl", re, sx) + einsum("cklm,mx->ckxl", im, cx),
        ]
    )
    re, im = lax.all_to_all(pair, "px", split_axis=3, concat_axis=4, tiled=True)
    pair = jnp.stack(
        [
            einsum("ckxl,ly->cxyk", re, cy) - einsum("ckxl,ly->cxyk", im, sy),
            einsum("ckxl,ly->cxyk", re, sy) + einsum("ckxl,ly->cxyk", im, cy),
        ]
    )
    re, im = lax.all_to_all(pair, "py", split_axis=3, concat_axis=4, tiled=True)
    return einsum("cxyk,kz->cxyz", re, f32((cz * scale).T)) - einsum(
        "cxyk,kz->cxyz", im, f32((sz * scale).T)
    )


def body(velocity, cotangent, weight_in, bias_in, weight_out):
    npx, npy = lax.axis_size("px"), lax.axis_size("py")
    _, nx, ny, NZ = velocity.shape
    sizes = (nx * npx, ny * npy, NZ)
    spacings = tuple(2.0 * math.pi / size for size in sizes)
    rows = rows_of(ny)

    def beside_first(velocity, weight_in, bias_in, weight_out):
        w1, bias = input_weights(weight_in, bias_in, ny, rows)
        w2, w3 = output_weights(weight_in, weight_out, ny, rows)
        wide = widened(velocity, *halo(velocity, "py", 2, 3))
        return (w1, bias, w2, w3, wide), halo(wide, "px", 1, 3)

    def beside_second(first, halo_first):
        w1, bias, w2, w3, wide = first
        low, up = halo_first
        vel_ext = jnp.concatenate([low, wide, up], axis=1)
        slope, grads = velocity_step(vel_ext, w1, bias, nx, ny, spacings)
        return vel_ext, slope, grads, w2, w3

    others = (velocity, weight_in, bias_in, weight_out)
    if (NZ // 2) % (npx * npy) == 0 and nx * (NZ // 2) % (npx * npy * LANES) == 0 and ny % 8 == 0:
        lam, second = projected_once(cotangent, sizes, npx, npy, others, beside_first, beside_second)
    else:
        lam = projected_twice(cotangent, sizes, npx, npy)
        second = beside_second(*beside_first(*others))
    vel_ext, slope, grads, w2, w3 = second
    return closure_step(vel_ext, bordered(lam), slope, grads, w2, w3, nx, ny, spacings)


def solution(mesh):
    placed = (P(None, "px", "py", None), P(None, "px", "py", None), P(), P(), P())
    return jax.shard_map(
        body, mesh=mesh, in_specs=placed, out_specs=P(None, "px", "py", None), check_vma=False
    )
```

```python
import functools
import math

import jax
import jax.numpy as jnp
import ml_dtypes
import numpy as np
from jax import lax
from jax.experimental import pallas as pl
from jax.experimental.pallas import tpu as pltpu
from jax.sharding import PartitionSpec as P

time_step = 0.005
high = lax.Precision.HIGH
LANES = 128
SIDES = 4
taps = ((1, 45.0), (2, -9.0), (3, 1.0))


def rows_of(ny):
    return -(-(ny + 6) // 8) * 8


def halo(block, axis, dim, width):
    count = lax.axis_size(axis)
    forward = [(i, (i + 1) % count) for i in range(count)]
    backward = [(target, source) for source, target in forward]
    low = lax.ppermute(
        lax.slice_in_dim(block, block.shape[dim] - width, None, axis=dim), axis, forward
    )
    high_side = lax.ppermute(lax.slice_in_dim(block, 0, width, axis=dim), axis, backward)
    return low, high_side


def widened(block, low, up):
    ny = block.shape[2]
    extra = rows_of(ny) - ny - 6
    parts = [block, up]
    if extra:
        parts.append(jnp.zeros(block.shape[:2] + (extra,) + block.shape[3:], block.dtype))
    return jnp.concatenate(parts + [low], axis=2)


def joined(low, wide, up):
    nx = wide.shape[1]
    extra = max(0, -(-(nx + 2) // SIDES) * SIDES - nx - 2)
    parts = [low, wide, up]
    if extra:
        parts.append(jnp.zeros(wide.shape[:1] + (extra,) + wide.shape[2:], wide.dtype))
    return jnp.concatenate(parts, axis=1)


def bordered(block):
    wide = widened(block, *halo(block, "py", 2, 3))
    low, up = halo(wide, "px", 1, 3)
    return joined(low, wide, up)


def zroll(value, shift):
    return pltpu.roll(value, shift % LANES, value.ndim - 1)


def many(count, size, run):
    @pl.loop(0, count // size)
    def _(block):
        for piece in range(size):
            run(block * size + piece)

    for last in range(count - count % size, count):
        run(last)


def velocity_kernel(sizes, vel, w1, b1, slope, grads, vs):
    nx, ny, rows, half, spacings = sizes
    vblock, out_rows = 9 * rows, w1.shape[0]

    def prepare(k):
        for side in range(SIDES):
            v = vel[:, k + 1 + side * half].reshape(3 * rows, LANES)
            for t in range(3):
                start = pl.multiple_of(k * vblock + t * 3 * rows, 16)
                vs[pl.ds(start, 3 * rows), side * LANES : (side + 1) * LANES] = zroll(
                    v, 1 - t
                ).astype(jnp.bfloat16)

    many(half + 2, 2, prepare)

    def step(i):
        pre = jnp.dot(
            w1[:, : 3 * vblock],
            vs[pl.ds(pl.multiple_of(i * vblock, 16), 3 * vblock), :],
            preferred_element_type=jnp.float32,
        )
        t = jnp.tanh(pre + b1[...])
        slope[pl.ds(pl.multiple_of(i * out_rows, 16), out_rows), :] = (1.0 - t * t).astype(
            jnp.bfloat16
        )

    many(half, 2, step)

    def gradient(x):
        e = x + 3
        for c in range(3):
            wide = vel[c, e]
            for b in range(3):
                total = 0.0
                for d, weight in taps:
                    if b == 0:
                        pair = vel[c, e + d, :ny] - vel[c, e - d, :ny]
                    elif b == 1:
                        pair = (pltpu.roll(wide, rows - d, 0) - pltpu.roll(wide, d, 0))[:ny]
                    else:
                        pair = zroll(wide[:ny], -d) - zroll(wide[:ny], d)
                    total += (weight / (60.0 * spacings[b])) * pair
                grads[3 * b + c, x] = total

    many(nx, 2, gradient)


def closure_kernel(sizes, vel, lam, slope, grads, w2, w3, out, ss, acc):
    nx, ny, rows, half, spacings = sizes
    sblock, hid_rows = 18 * rows, w2.shape[0]
    inv2 = [1.0 / (2.0 * h) for h in spacings]

    def prepare(k):
        for side in range(SIDES):
            e = k + 1 + side * half
            lanes = slice(side * LANES, (side + 1) * LANES)
            l = [lam[c, e] for c in range(3)]
            dx = [(lam[c, e + 1] - lam[c, e - 1]) * inv2[0] for c in range(3)]
            dy = [
                (pltpu.roll(l[c], rows - 1, 0) - pltpu.roll(l[c], 1, 0)) * inv2[1]
                for c in range(3)
            ]
            dz = [(zroll(l[c], -1) - zroll(l[c], 1)) * inv2[2] for c in range(3)]
            s = jnp.concatenate(
                [dx[0], dy[1], dz[2], dy[0] + dx[1], dz[0] + dx[2], dz[1] + dy[2]], axis=0
            )
            for t in range(3):
                start = pl.multiple_of(k * sblock + t * 6 * rows, 16)
                ss[pl.ds(start, 6 * rows), lanes] = zroll(s, 1 - t).astype(jnp.bfloat16)
        acc[k] = jnp.zeros(acc.shape[1:], acc.dtype)

    many(half + 2, 2, prepare)

    def step(i):
        hid = jnp.dot(
            w2[:, : 3 * sblock],
            ss[pl.ds(pl.multiple_of(i * sblock, 16), 3 * sblock), :],
            preferred_element_type=jnp.float32,
        )
        part = slope[pl.ds(pl.multiple_of(i * hid_rows, 16), hid_rows), :]
        p = (hid * part.astype(jnp.float32)).astype(jnp.bfloat16)
        c = jnp.dot(w3[...], p, preferred_element_type=jnp.float32)
        for d in range(3):
            acc[i + d] += c[d * 9 * ny : (d + 1) * 9 * ny]

    many(half, 2, step)

    for d in range(2):
        acc[half + d, :, : (SIDES - 1) * LANES] += acc[d, :, LANES:]

    def finish(x, idx, side):
        e = x + 3
        lanes = slice(side * LANES, (side + 1) * LANES)
        low = [acc[idx, d * 3 * ny : (d + 1) * 3 * ny, lanes] for d in range(3)]
        closure = zroll(low[0], -1) + low[1] + zroll(low[2], 1)
        wide = [lam[c, e] for c in range(3)]
        l0 = [value[:ny] for value in wide]
        vy = vel[1, e]
        vz = vel[2, e, :ny]
        vx = {q: vel[0, e + q, :ny] for d, _ in taps for q in (d, -d)}
        for c in range(3):
            total = closure[c * ny : (c + 1) * ny]
            ly = wide[c] * vy
            lz = l0[c] * vz
            for d, weight in taps:
                fx = lam[c, e + d, :ny] * vx[d] - lam[c, e - d, :ny] * vx[-d]
                fy = (pltpu.roll(ly, rows - d, 0) - pltpu.roll(ly, d, 0))[:ny]
                fz = zroll(lz, -d) - zroll(lz, d)
                for b, pair in enumerate((fx, fy, fz)):
                    total += (weight / (60.0 * spacings[b])) * pair
            for a in range(3):
                total -= l0[a] * grads[3 * c + a, x]
            out[c, x] = l0[c] + time_step * total

    shared = nx - (SIDES - 1) * half

    @pl.loop(0, shared)
    def _(x):
        for side in range(SIDES):
            finish(x + side * half, x + 2, side)

    @pl.loop(shared, half)
    def _(x):
        for side in range(SIDES - 1):
            finish(x + side * half, x + 2, side)


def lane_padded(size):
    return -(-size // LANES) * LANES


def banded_table(channels, ny, rows):
    table = np.zeros((channels, 3, 3, 3, ny + 2, 3, 3, channels, rows), np.float32)
    for c in range(channels):
        for x in range(3):
            for d in range(3):
                for z in range(3):
                    for p in range(ny + 2):
                        table[c, x, d, z, p, x, z, c, (p + d - 2) % rows] = 1.0
    table = table.reshape(27 * channels, ny + 2, 9 * channels * rows)
    extra = lane_padded(table.shape[2]) - table.shape[2]
    return np.pad(table, ((0, 0), (0, 0), (0, extra)))


def returned_table(channels, ny):
    table = np.zeros((channels, 3, 3, 3, ny + 2, 3, 3, channels, ny), np.float32)
    for c in range(channels):
        for x in range(3):
            for d in range(3):
                for z in range(3):
                    for y in range(ny):
                        table[c, x, d, z, y + 2 - d, x, z, c, y] = 1.0
    table = table.reshape(27 * channels, ny + 2, 9 * channels * ny)
    extra = lane_padded(table.shape[2]) - table.shape[2]
    return np.pad(table, ((0, 0), (0, 0), (0, extra)))


def spread(weight, table):
    flat = table.reshape(table.shape[0], -1)
    wide = jnp.dot(
        weight, jnp.asarray(flat, jnp.bfloat16), preferred_element_type=jnp.float32
    ).astype(jnp.bfloat16)
    columns = table.shape[2]
    return jnp.concatenate(
        [wide[:, p * columns : (p + 1) * columns] for p in range(table.shape[1])], axis=0
    )


def input_weights(weight_in, bias_in, ny, rows):
    hid, comp = weight_in.shape[:2]
    w1 = spread(weight_in.reshape(hid, -1), banded_table(comp, ny, rows))
    return w1, jnp.tile(bias_in, ny + 2)[:, None]


def output_weights(weight_in, weight_out, ny, rows):
    hid, comp = weight_in.shape[:2]
    flipped = jnp.flip(weight_out, (2, 3, 4)).transpose(1, 0, 2, 3, 4).reshape(hid, -1)
    w2 = spread(flipped, banded_table(weight_out.shape[0], ny, rows))
    w3 = spread(weight_in.reshape(hid, -1), returned_table(comp, ny)).T[: 9 * comp * ny]
    return w2, w3


def velocity_step(vel_ext, w1, bias, nx, ny, spacings):
    rows = vel_ext.shape[2]
    half = -(-(nx + 2) // SIDES)
    vm = pl.BlockSpec(memory_space=pltpu.VMEM)
    return pl.pallas_call(
        functools.partial(velocity_kernel, (nx, ny, rows, half, spacings)),
        out_shape=(
            jax.ShapeDtypeStruct((half * w1.shape[0], SIDES * LANES), jnp.bfloat16),
            jax.ShapeDtypeStruct((9, nx, ny, LANES), jnp.float32),
        ),
        in_specs=[vm] * 3,
        out_specs=(vm, vm),
        scratch_shapes=[pltpu.VMEM(((half + 2) * 9 * rows, SIDES * LANES), jnp.bfloat16)],
        compiler_params=pltpu.CompilerParams(vmem_limit_bytes=20 * 2**20),
        cost_estimate=pl.CostEstimate(
            flops=2 * half * w1.shape[0] * w1.shape[1] * SIDES * LANES,
            bytes_accessed=12 * 2**20,
            transcendentals=half * w1.shape[0] * SIDES * LANES,
        ),
        name="velocity",
    )(vel_ext, w1, bias)


def closure_step(vel_ext, lam_ext, slope, grads, w2, w3, nx, ny, spacings):
    rows = vel_ext.shape[2]
    half = -(-(nx + 2) // SIDES)
    vm = pl.BlockSpec(memory_space=pltpu.VMEM)
    return pl.pallas_call(
        functools.partial(closure_kernel, (nx, ny, rows, half, spacings)),
        out_shape=jax.ShapeDtypeStruct((3, nx, ny, LANES), jnp.float32),
        in_specs=[vm] * 6,
        out_specs=vm,
        scratch_shapes=[
            pltpu.VMEM(((half + 2) * 18 * rows, SIDES * LANES), jnp.bfloat16),
            pltpu.VMEM((half + 2, 9 * ny, SIDES * LANES), jnp.float32),
        ],
        compiler_params=pltpu.CompilerParams(vmem_limit_bytes=28 * 2**20),
        name="closure",
    )(vel_ext, lam_ext, slope, grads, w2, w3)


def waves(length, modes):
    products = np.arange(length)[:, None] * np.arange(modes)[None, :] % length
    phases = products.astype(np.float64) * (2.0 * math.pi / length)
    return np.cos(phases), np.sin(phases)


def f32(table):
    return jnp.asarray(np.asarray(table, np.float32))


def project(re, im, index_x, index_y, index_z, sizes):
    NX, NY, NZ = sizes

    def signed(index, length):
        return jnp.where(index > length // 2, index - length, index).astype(jnp.float32)

    wx, wy, wz = signed(index_x, NX), signed(index_y, NY), signed(index_z, NZ)
    squared = wx * wx + wy * wy + wz * wz
    keep = (index_x != NX // 2) & (index_y != NY // 2) & (index_z != NZ // 2)
    inverse = jnp.where(squared > 0, 1.0 / jnp.maximum(squared, 1.0), 0.0)
    done = []
    for part in (re, im):
        dotted = (wx * part[0] + wy * part[1] + wz * part[2]) * inverse
        done.append([jnp.where(keep, part[c] - w * dotted, 0.0) for c, w in enumerate((wx, wy, wz))])
    return jnp.stack(done[0]), jnp.stack(done[1])


def einsum(*args):
    return jnp.einsum(*args, precision=high)


def mode_weights(NX, NY, NZ):
    scale = np.full((NZ // 2,), 2.0 / (NX * NY * NZ))
    scale[0] /= 2.0
    return scale


def halves(table):
    table = np.asarray(table, np.float32)
    first = table.astype(ml_dtypes.bfloat16)
    second = (table - first.astype(np.float32)).astype(ml_dtypes.bfloat16)
    return jnp.asarray(np.stack([first, second]))


def cut(value):
    first = value.astype(jnp.bfloat16)
    return first, (value - first.astype(jnp.float32)).astype(jnp.bfloat16)


def dot3(left, right, dims=((1,), (0,))):
    def one(a, b):
        return lax.dot_general(a, b, (dims, ((), ())), preferred_element_type=jnp.float32)

    return one(left[0], right[0]) + (one(left[0], right[1]) + one(left[1], right[0]))


def forward_kernel(sizes, cot, table, sent):
    total, nj, nx, ny = sizes
    left = (table[0], table[1])
    for c in range(3):
        planes = []
        for y in range(ny):
            modes = dot3(left, cut(cot[c, :, y, :]), ((1,), (1,)))
            rows = 2 * total
            planes.append(
                jnp.concatenate([modes[j * rows : (j + 1) * rows] for j in range(nj)], axis=1)
            )
        block = jnp.swapaxes(jnp.stack(planes), 0, 1)
        sent[:, :, c] = block.reshape(total, 2, ny, nj * nx)


def backward_kernel(sizes, got, table, lam):
    total, nj, nx, ny = sizes
    right = (table[0], table[1])
    for c in range(3):
        block = got[:, :, c].reshape(2 * total, ny, nj * nx)
        block = jnp.swapaxes(block, 0, 1)
        for y in range(ny):
            modes = jnp.concatenate(
                [block[y][:, j * nx : (j + 1) * nx] for j in range(nj)], axis=0
            )
            lam[c, :, y, :] = dot3(cut(modes), right, ((0,), (0,)))


def middle_kernel(sizes, got, lanes, fy, fx, bx, by, sent):
    npx, npy, ny, NY, wide = sizes
    rows = 2 * npy * ny
    per = wide // npx

    def table(ref):
        return ref[0], ref[1]

    modes = []
    for c in range(3):
        block = jnp.concatenate(
            [got[h * npy : (h + 1) * npy, :, c].reshape(rows, per) for h in range(npx)], axis=1
        )
        mixed = dot3(table(fy), cut(block))
        both = dot3(cut(mixed), table(fx))
        re = both[:NY, :wide] + both[NY:, wide:]
        im = both[NY:, :wide] - both[:NY, wide:]
        modes.append((re, im))
    ky = lax.broadcasted_iota(jnp.int32, (NY, wide), 0)
    wy = jnp.where(ky > NY // 2, ky - NY, ky).astype(jnp.float32)
    wx, wz = lanes[0:1], lanes[1:2]
    keep = jnp.where(ky == NY // 2, 0.0, 1.0) * lanes[2:3]
    squared = wx * wx + wy * wy + wz * wz
    inverse = jnp.where(squared > 0, 1.0 / jnp.maximum(squared, 1.0), 0.0)
    dotted = [
        (wx * modes[0][r] + wy * modes[1][r] + wz * modes[2][r]) * inverse for r in range(2)
    ]
    for c, w in enumerate((wx, wy, wz)):
        pair = jnp.concatenate([(modes[c][r] - w * dotted[r]) * keep for r in range(2)], axis=0)
        both = dot3(cut(pair), table(bx))
        re = both[:NY, :wide] - both[NY:, wide:]
        im = both[NY:, :wide] + both[:NY, wide:]
        back = dot3(table(by), cut(jnp.concatenate([re, im], axis=0)))
        for h in range(npx):
            sent[h * npy : (h + 1) * npy, :, c] = back[:, h * per : (h + 1) * per].reshape(
                npy, 2, ny, per
            )


def local_call(kernel, shape, name, *operands):
    vm = pl.BlockSpec(memory_space=pltpu.VMEM)
    return pl.pallas_call(
        kernel,
        out_shape=jax.ShapeDtypeStruct(shape, jnp.float32),
        in_specs=[vm] * len(operands),
        out_specs=vm,
        compiler_params=pltpu.CompilerParams(vmem_limit_bytes=40 * 2**20),
        name=name,
    )(*operands)


def projected_once(cotangent, sizes, npx, npy, others, beside_first, beside_second):
    NX, NY, NZ = sizes
    _, nx, ny, _ = cotangent.shape
    total = npx * npy
    nj = NZ // 2 // total
    cz, sz = waves(NZ, NZ // 2)
    cy, sy = waves(NY, NY)
    cx, sx = waves(NX, NX)
    shape = (total, 2, 3, ny, nj * nx)
    forward_z = np.stack([cz, -sz], 0).reshape(2, NZ, total, nj)
    forward_z = forward_z.transpose(3, 2, 0, 1).reshape(NZ, NZ)
    sent = local_call(
        functools.partial(forward_kernel, (total, nj, nx, ny)),
        shape,
        "forward",
        cotangent,
        halves(forward_z),
    )
    sent, others = lax.optimization_barrier((sent, others))
    got = lax.all_to_all(sent, ("px", "py"), 0, 0, tiled=True)
    first, halo_first = beside_first(*others)
    got, first = lax.optimization_barrier((got, first))
    forward_y = np.stack([np.stack([cy, -sy], 0), np.stack([sy, cy], 0)], 0)
    forward_y = forward_y.reshape(2, 2, npy, ny, NY).transpose(1, 4, 2, 0, 3)
    eye = np.eye(nj)
    forward_x = np.stack([cx, sx], 0).reshape(2, npx, nx, NX)
    forward_x = np.einsum("shxm,jk->hjxskm", forward_x, eye)
    backward_x = np.stack([cx, sx], 0).reshape(2, NX, npx, nx)
    backward_x = np.einsum("smhx,jk->jmshkx", backward_x, eye)
    backward_y = np.stack([np.stack([cy, sy], 0), np.stack([-sy, cy], 0)], 0)
    backward_y = backward_y.reshape(2, 2, NY, npy, ny).transpose(3, 1, 4, 0, 2)
    wide = nj * NX
    me = lax.axis_index("px") * npy + lax.axis_index("py")
    lane = jnp.arange(wide, dtype=jnp.int32)
    index_x, index_z = lane % NX, me * nj + lane // NX
    wave_x = jnp.where(index_x > NX // 2, index_x - NX, index_x).astype(jnp.float32)
    keep = ((index_x != NX // 2) & (index_z != NZ // 2)).astype(jnp.float32)
    lanes = jnp.stack([wave_x, index_z.astype(jnp.float32), keep])
    sent = local_call(
        functools.partial(middle_kernel, (npx, npy, ny, NY, wide)),
        shape,
        "middle",
        got,
        lanes,
        halves(forward_y.reshape(2 * NY, 2 * NY)),
        halves(forward_x.reshape(wide, 2 * wide)),
        halves(backward_x.reshape(wide, 2 * wide)),
        halves(backward_y.reshape(2 * NY, 2 * NY)),
    )
    sent, first, halo_first = lax.optimization_barrier((sent, first, halo_first))
    got = lax.all_to_all(sent, ("px", "py"), 0, 0, tiled=True)
    got, second = lax.optimization_barrier((got, beside_second(first, halo_first)))
    scale = mode_weights(NX, NY, NZ)
    backward_z = np.stack([(cz * scale).T, (-sz * scale).T], 0).reshape(2, total, nj, NZ)
    backward_z = backward_z.transpose(2, 1, 0, 3).reshape(NZ, NZ)
    lam = local_call(
        functools.partial(backward_kernel, (total, nj, nx, ny)),
        cotangent.shape,
        "backward",
        got,
        halves(backward_z),
    )
    return lam, second


def projected_twice(cotangent, sizes, npx, npy):
    NX, NY, NZ = sizes
    cz, sz = waves(NZ, NZ // 2)
    cy, sy = map(f32, waves(NY, NY))
    cx, sx = map(f32, waves(NX, NX))
    scale = mode_weights(NX, NY, NZ)
    stacked = jnp.stack(
        [einsum("cxyz,zk->cxyk", cotangent, f32(cz)), einsum("cxyz,zk->cxyk", cotangent, f32(-sz))]
    )
    re, im = lax.all_to_all(stacked, "py", split_axis=4, concat_axis=3, tiled=True)
    pair = jnp.stack(
        [
            einsum("cxyk,yl->ckxl", re, cy) + einsum("cxyk,yl->ckxl", im, sy),
            einsum("cxyk,yl->ckxl", im, cy) - einsum("cxyk,yl->ckxl", re, sy),
        ]
    )
    re, im = lax.all_to_all(pair, "px", split_axis=4, concat_axis=3, tiled=True)
    re, im = (
        einsum("ckxl,xm->cklm", re, cx) + einsum("ckxl,xm->cklm", im, sx),
        einsum("ckxl,xm->cklm", im, cx) - einsum("ckxl,xm->cklm", re, sx),
    )
    nk, nl = re.shape[1], re.shape[2]
    index_z = (lax.axis_index("py") * nk + jnp.arange(nk, dtype=jnp.int32))[:, None, None]
    index_y = (lax.axis_index("px") * nl + jnp.arange(nl, dtype=jnp.int32))[None, :, None]
    index_x = jnp.arange(NX, dtype=jnp.int32)[None, None, :]
    re, im = project(re, im, index_x, index_y, index_z, sizes)
    pair = jnp.stack(
        [
            einsum("cklm,mx->ckxl", re, cx) - einsum("cklm,mx->ckxl", im, sx),
            einsum("cklm,mx->ckxl", re, sx) + einsum("cklm,mx->ckxl", im, cx),
        ]
    )
    re, im = lax.all_to_all(pair, "px", split_axis=3, concat_axis=4, tiled=True)
    pair = jnp.stack(
        [
            einsum("ckxl,ly->cxyk", re, cy) - einsum("ckxl,ly->cxyk", im, sy),
            einsum("ckxl,ly->cxyk", re, sy) + einsum("ckxl,ly->cxyk", im, cy),
        ]
    )
    re, im = lax.all_to_all(pair, "py", split_axis=3, concat_axis=4, tiled=True)
    return einsum("cxyk,kz->cxyz", re, f32((cz * scale).T)) - einsum(
        "cxyk,kz->cxyz", im, f32((sz * scale).T)
    )


def body(velocity, cotangent, weight_in, bias_in, weight_out):
    npx, npy = lax.axis_size("px"), lax.axis_size("py")
    _, nx, ny, NZ = velocity.shape
    sizes = (nx * npx, ny * npy, NZ)
    spacings = tuple(2.0 * math.pi / size for size in sizes)
    rows = rows_of(ny)

    def beside_first(velocity, weight_in, bias_in, weight_out):
        w1, bias = input_weights(weight_in, bias_in, ny, rows)
        w2, w3 = output_weights(weight_in, weight_out, ny, rows)
        wide = widened(velocity, *halo(velocity, "py", 2, 3))
        return (w1, bias, w2, w3, wide), halo(wide, "px", 1, 3)

    def beside_second(first, halo_first):
        w1, bias, w2, w3, wide = first
        low, up = halo_first
        vel_ext = joined(low, wide, up)
        slope, grads = velocity_step(vel_ext, w1, bias, nx, ny, spacings)
        return vel_ext, slope, grads, w2, w3

    others = (velocity, weight_in, bias_in, weight_out)
    if (NZ // 2) % (npx * npy) == 0 and nx * (NZ // 2) % (npx * npy * LANES) == 0 and ny % 8 == 0:
        lam, second = projected_once(cotangent, sizes, npx, npy, others, beside_first, beside_second)
    else:
        lam = projected_twice(cotangent, sizes, npx, npy)
        second = beside_second(*beside_first(*others))
    vel_ext, slope, grads, w2, w3 = second
    return closure_step(vel_ext, bordered(lam), slope, grads, w2, w3, nx, ny, spacings)


def solution(mesh):
    placed = (P(None, "px", "py", None), P(None, "px", "py", None), P(), P(), P())
    return jax.shard_map(
        body, mesh=mesh, in_specs=placed, out_specs=P(None, "px", "py", None), check_vma=False
    )
```

```python
import functools
import math

import jax
import jax.numpy as jnp
import ml_dtypes
import numpy as np
from jax import lax
from jax.experimental import pallas as pl
from jax.experimental.pallas import tpu as pltpu
from jax.sharding import PartitionSpec as P

time_step = 0.005
high = lax.Precision.HIGH
LANES = 128
SIDES = 6
taps = ((1, 45.0), (2, -9.0), (3, 1.0))


def rows_of(ny):
    return -(-(ny + 6) // 8) * 8


def halo(block, axis, dim, width):
    count = lax.axis_size(axis)
    forward = [(i, (i + 1) % count) for i in range(count)]
    backward = [(target, source) for source, target in forward]
    low = lax.ppermute(
        lax.slice_in_dim(block, block.shape[dim] - width, None, axis=dim), axis, forward
    )
    high_side = lax.ppermute(lax.slice_in_dim(block, 0, width, axis=dim), axis, backward)
    return low, high_side


def widened(block, low, up):
    ny = block.shape[2]
    extra = rows_of(ny) - ny - 6
    parts = [block, up]
    if extra:
        parts.append(jnp.zeros(block.shape[:2] + (extra,) + block.shape[3:], block.dtype))
    return jnp.concatenate(parts + [low], axis=2)


def joined(low, wide, up):
    nx = wide.shape[1]
    extra = max(0, -(-(nx + 2) // SIDES) * SIDES - nx - 2)
    parts = [low, wide, up]
    if extra:
        parts.append(jnp.zeros(wide.shape[:1] + (extra,) + wide.shape[2:], wide.dtype))
    return jnp.concatenate(parts, axis=1)


def bordered(block):
    wide = widened(block, *halo(block, "py", 2, 3))
    low, up = halo(wide, "px", 1, 3)
    return joined(low, wide, up)


def zroll(value, shift):
    return pltpu.roll(value, shift % LANES, value.ndim - 1)


def many(count, size, run):
    @pl.loop(0, count // size)
    def _(block):
        for piece in range(size):
            run(block * size + piece)

    for last in range(count - count % size, count):
        run(last)


def velocity_kernel(sizes, vel, w1, b1, slope, grads, vs):
    nx, ny, rows, half, spacings = sizes
    vblock, out_rows = 9 * rows, w1.shape[0]

    def prepare(k):
        for side in range(SIDES):
            v = vel[:, k + 1 + side * half].reshape(3 * rows, LANES)
            for t in range(3):
                start = pl.multiple_of(k * vblock + t * 3 * rows, 16)
                vs[pl.ds(start, 3 * rows), side * LANES : (side + 1) * LANES] = zroll(
                    v, 1 - t
                ).astype(jnp.bfloat16)

    many(half + 2, 2, prepare)

    def step(i):
        pre = jnp.dot(
            w1[:, : 3 * vblock],
            vs[pl.ds(pl.multiple_of(i * vblock, 16), 3 * vblock), :],
            preferred_element_type=jnp.float32,
        )
        t = jnp.tanh(pre + b1[...])
        slope[pl.ds(pl.multiple_of(i * out_rows, 16), out_rows), :] = (1.0 - t * t).astype(
            jnp.bfloat16
        )

    many(half, 2, step)

    def gradient(x):
        e = x + 3
        for c in range(3):
            wide = vel[c, e]
            for b in range(3):
                total = 0.0
                for d, weight in taps:
                    if b == 0:
                        pair = vel[c, e + d, :ny] - vel[c, e - d, :ny]
                    elif b == 1:
                        pair = (pltpu.roll(wide, rows - d, 0) - pltpu.roll(wide, d, 0))[:ny]
                    else:
                        pair = zroll(wide[:ny], -d) - zroll(wide[:ny], d)
                    total += (weight / (60.0 * spacings[b])) * pair
                grads[3 * b + c, x] = total

    many(nx, 2, gradient)


def closure_kernel(sizes, vel, lam, slope, grads, w2, w3, out, ss, acc):
    nx, ny, rows, half, spacings = sizes
    sblock, hid_rows = 18 * rows, w2.shape[0]
    inv2 = [1.0 / (2.0 * h) for h in spacings]

    def prepare(k):
        for side in range(SIDES):
            e = k + 1 + side * half
            lanes = slice(side * LANES, (side + 1) * LANES)
            l = [lam[c, e] for c in range(3)]
            dx = [(lam[c, e + 1] - lam[c, e - 1]) * inv2[0] for c in range(3)]
            dy = [
                (pltpu.roll(l[c], rows - 1, 0) - pltpu.roll(l[c], 1, 0)) * inv2[1]
                for c in range(3)
            ]
            dz = [(zroll(l[c], -1) - zroll(l[c], 1)) * inv2[2] for c in range(3)]
            s = jnp.concatenate(
                [dx[0], dy[1], dz[2], dy[0] + dx[1], dz[0] + dx[2], dz[1] + dy[2]], axis=0
            )
            for t in range(3):
                start = pl.multiple_of(k * sblock + t * 6 * rows, 16)
                ss[pl.ds(start, 6 * rows), lanes] = zroll(s, 1 - t).astype(jnp.bfloat16)
        acc[k] = jnp.zeros(acc.shape[1:], acc.dtype)

    many(half + 2, 2, prepare)

    def step(i):
        hid = jnp.dot(
            w2[:, : 3 * sblock],
            ss[pl.ds(pl.multiple_of(i * sblock, 16), 3 * sblock), :],
            preferred_element_type=jnp.float32,
        )
        part = slope[pl.ds(pl.multiple_of(i * hid_rows, 16), hid_rows), :]
        p = (hid * part.astype(jnp.float32)).astype(jnp.bfloat16)
        c = jnp.dot(w3[...], p, preferred_element_type=jnp.float32)
        for d in range(3):
            acc[i + d] += c[d * 9 * ny : (d + 1) * 9 * ny]

    many(half, 2, step)

    for d in range(2):
        acc[half + d, :, : (SIDES - 1) * LANES] += acc[d, :, LANES:]

    def finish(x, idx, side):
        e = x + 3
        lanes = slice(side * LANES, (side + 1) * LANES)
        low = [acc[idx, d * 3 * ny : (d + 1) * 3 * ny, lanes] for d in range(3)]
        closure = zroll(low[0], -1) + low[1] + zroll(low[2], 1)
        wide = [lam[c, e] for c in range(3)]
        l0 = [value[:ny] for value in wide]
        vy = vel[1, e]
        vz = vel[2, e, :ny]
        vx = {q: vel[0, e + q, :ny] for d, _ in taps for q in (d, -d)}
        for c in range(3):
            total = closure[c * ny : (c + 1) * ny]
            ly = wide[c] * vy
            lz = l0[c] * vz
            for d, weight in taps:
                fx = lam[c, e + d, :ny] * vx[d] - lam[c, e - d, :ny] * vx[-d]
                fy = (pltpu.roll(ly, rows - d, 0) - pltpu.roll(ly, d, 0))[:ny]
                fz = zroll(lz, -d) - zroll(lz, d)
                for b, pair in enumerate((fx, fy, fz)):
                    total += (weight / (60.0 * spacings[b])) * pair
            for a in range(3):
                total -= l0[a] * grads[3 * c + a, x]
            out[c, x] = l0[c] + time_step * total

    shared = nx - (SIDES - 1) * half

    @pl.loop(0, shared)
    def _(x):
        for side in range(SIDES):
            finish(x + side * half, x + 2, side)

    @pl.loop(shared, half)
    def _(x):
        for side in range(SIDES - 1):
            finish(x + side * half, x + 2, side)


def lane_padded(size):
    return -(-size // LANES) * LANES


def banded_table(channels, ny, rows):
    table = np.zeros((channels, 3, 3, 3, ny + 2, 3, 3, channels, rows), np.float32)
    for c in range(channels):
        for x in range(3):
            for d in range(3):
                for z in range(3):
                    for p in range(ny + 2):
                        table[c, x, d, z, p, x, z, c, (p + d - 2) % rows] = 1.0
    table = table.reshape(27 * channels, ny + 2, 9 * channels * rows)
    extra = lane_padded(table.shape[2]) - table.shape[2]
    return np.pad(table, ((0, 0), (0, 0), (0, extra)))


def returned_table(channels, ny):
    table = np.zeros((channels, 3, 3, 3, ny + 2, 3, 3, channels, ny), np.float32)
    for c in range(channels):
        for x in range(3):
            for d in range(3):
                for z in range(3):
                    for y in range(ny):
                        table[c, x, d, z, y + 2 - d, x, z, c, y] = 1.0
    table = table.reshape(27 * channels, ny + 2, 9 * channels * ny)
    extra = lane_padded(table.shape[2]) - table.shape[2]
    return np.pad(table, ((0, 0), (0, 0), (0, extra)))


def spread(weight, table):
    flat = table.reshape(table.shape[0], -1)
    wide = jnp.dot(
        weight, jnp.asarray(flat, jnp.bfloat16), preferred_element_type=jnp.float32
    ).astype(jnp.bfloat16)
    columns = table.shape[2]
    return jnp.concatenate(
        [wide[:, p * columns : (p + 1) * columns] for p in range(table.shape[1])], axis=0
    )


def input_weights(weight_in, bias_in, ny, rows):
    hid, comp = weight_in.shape[:2]
    w1 = spread(weight_in.reshape(hid, -1), banded_table(comp, ny, rows))
    return w1, jnp.tile(bias_in, ny + 2)[:, None]


def output_weights(weight_in, weight_out, ny, rows):
    hid, comp = weight_in.shape[:2]
    flipped = jnp.flip(weight_out, (2, 3, 4)).transpose(1, 0, 2, 3, 4).reshape(hid, -1)
    w2 = spread(flipped, banded_table(weight_out.shape[0], ny, rows))
    w3 = spread(weight_in.reshape(hid, -1), returned_table(comp, ny)).T[: 9 * comp * ny]
    return w2, w3


def velocity_step(vel_ext, w1, bias, nx, ny, spacings):
    rows = vel_ext.shape[2]
    half = -(-(nx + 2) // SIDES)
    vm = pl.BlockSpec(memory_space=pltpu.VMEM)
    return pl.pallas_call(
        functools.partial(velocity_kernel, (nx, ny, rows, half, spacings)),
        out_shape=(
            jax.ShapeDtypeStruct((half * w1.shape[0], SIDES * LANES), jnp.bfloat16),
            jax.ShapeDtypeStruct((9, nx, ny, LANES), jnp.float32),
        ),
        in_specs=[vm] * 3,
        out_specs=(vm, vm),
        scratch_shapes=[pltpu.VMEM(((half + 2) * 9 * rows, SIDES * LANES), jnp.bfloat16)],
        compiler_params=pltpu.CompilerParams(vmem_limit_bytes=20 * 2**20),
        cost_estimate=pl.CostEstimate(
            flops=2 * half * w1.shape[0] * w1.shape[1] * SIDES * LANES,
            bytes_accessed=12 * 2**20,
            transcendentals=half * w1.shape[0] * SIDES * LANES,
        ),
        name="velocity",
    )(vel_ext, w1, bias)


def closure_step(vel_ext, lam_ext, slope, grads, w2, w3, nx, ny, spacings):
    rows = vel_ext.shape[2]
    half = -(-(nx + 2) // SIDES)
    vm = pl.BlockSpec(memory_space=pltpu.VMEM)
    return pl.pallas_call(
        functools.partial(closure_kernel, (nx, ny, rows, half, spacings)),
        out_shape=jax.ShapeDtypeStruct((3, nx, ny, LANES), jnp.float32),
        in_specs=[vm] * 6,
        out_specs=vm,
        scratch_shapes=[
            pltpu.VMEM(((half + 2) * 18 * rows, SIDES * LANES), jnp.bfloat16),
            pltpu.VMEM((half + 2, 9 * ny, SIDES * LANES), jnp.float32),
        ],
        compiler_params=pltpu.CompilerParams(vmem_limit_bytes=28 * 2**20),
        name="closure",
    )(vel_ext, lam_ext, slope, grads, w2, w3)


def waves(length, modes):
    products = np.arange(length)[:, None] * np.arange(modes)[None, :] % length
    phases = products.astype(np.float64) * (2.0 * math.pi / length)
    return np.cos(phases), np.sin(phases)


def f32(table):
    return jnp.asarray(np.asarray(table, np.float32))


def project(re, im, index_x, index_y, index_z, sizes):
    NX, NY, NZ = sizes

    def signed(index, length):
        return jnp.where(index > length // 2, index - length, index).astype(jnp.float32)

    wx, wy, wz = signed(index_x, NX), signed(index_y, NY), signed(index_z, NZ)
    squared = wx * wx + wy * wy + wz * wz
    keep = (index_x != NX // 2) & (index_y != NY // 2) & (index_z != NZ // 2)
    inverse = jnp.where(squared > 0, 1.0 / jnp.maximum(squared, 1.0), 0.0)
    done = []
    for part in (re, im):
        dotted = (wx * part[0] + wy * part[1] + wz * part[2]) * inverse
        done.append([jnp.where(keep, part[c] - w * dotted, 0.0) for c, w in enumerate((wx, wy, wz))])
    return jnp.stack(done[0]), jnp.stack(done[1])


def einsum(*args):
    return jnp.einsum(*args, precision=high)


def mode_weights(NX, NY, NZ):
    scale = np.full((NZ // 2,), 2.0 / (NX * NY * NZ))
    scale[0] /= 2.0
    return scale


def halves(table):
    table = np.asarray(table, np.float32)
    first = table.astype(ml_dtypes.bfloat16)
    second = (table - first.astype(np.float32)).astype(ml_dtypes.bfloat16)
    return jnp.asarray(np.stack([first, second]))


def cut(value):
    first = value.astype(jnp.bfloat16)
    return first, (value - first.astype(jnp.float32)).astype(jnp.bfloat16)


def dot3(left, right, dims=((1,), (0,))):
    def one(a, b):
        return lax.dot_general(a, b, (dims, ((), ())), preferred_element_type=jnp.float32)

    return one(left[0], right[0]) + (one(left[0], right[1]) + one(left[1], right[0]))


def forward_kernel(sizes, cot, table, sent):
    total, nj, nx, ny = sizes
    left = (table[0], table[1])
    for c in range(3):
        planes = []
        for y in range(ny):
            modes = dot3(left, cut(cot[c, :, y, :]), ((1,), (1,)))
            rows = 2 * total
            planes.append(
                jnp.concatenate([modes[j * rows : (j + 1) * rows] for j in range(nj)], axis=1)
            )
        block = jnp.swapaxes(jnp.stack(planes), 0, 1)
        sent[:, :, c] = block.reshape(total, 2, ny, nj * nx)


def backward_kernel(sizes, got, table, lam):
    total, nj, nx, ny = sizes
    right = (table[0], table[1])
    for c in range(3):
        block = got[:, :, c].reshape(2 * total, ny, nj * nx)
        block = jnp.swapaxes(block, 0, 1)
        for y in range(ny):
            modes = jnp.concatenate(
                [block[y][:, j * nx : (j + 1) * nx] for j in range(nj)], axis=0
            )
            lam[c, :, y, :] = dot3(cut(modes), right, ((0,), (0,)))


def middle_kernel(sizes, got, lanes, fy, fx, bx, by, sent):
    npx, npy, ny, NY, wide = sizes
    rows = 2 * npy * ny
    per = wide // npx

    def table(ref):
        return ref[0], ref[1]

    modes = []
    for c in range(3):
        block = jnp.concatenate(
            [got[h * npy : (h + 1) * npy, :, c].reshape(rows, per) for h in range(npx)], axis=1
        )
        mixed = dot3(table(fy), cut(block))
        both = dot3(cut(mixed), table(fx))
        re = both[:NY, :wide] + both[NY:, wide:]
        im = both[NY:, :wide] - both[:NY, wide:]
        modes.append((re, im))
    ky = lax.broadcasted_iota(jnp.int32, (NY, wide), 0)
    wy = jnp.where(ky > NY // 2, ky - NY, ky).astype(jnp.float32)
    wx, wz = lanes[0:1], lanes[1:2]
    keep = jnp.where(ky == NY // 2, 0.0, 1.0) * lanes[2:3]
    squared = wx * wx + wy * wy + wz * wz
    inverse = jnp.where(squared > 0, 1.0 / jnp.maximum(squared, 1.0), 0.0)
    dotted = [
        (wx * modes[0][r] + wy * modes[1][r] + wz * modes[2][r]) * inverse for r in range(2)
    ]
    for c, w in enumerate((wx, wy, wz)):
        pair = jnp.concatenate([(modes[c][r] - w * dotted[r]) * keep for r in range(2)], axis=0)
        both = dot3(cut(pair), table(bx))
        re = both[:NY, :wide] - both[NY:, wide:]
        im = both[NY:, :wide] + both[:NY, wide:]
        back = dot3(table(by), cut(jnp.concatenate([re, im], axis=0)))
        for h in range(npx):
            sent[h * npy : (h + 1) * npy, :, c] = back[:, h * per : (h + 1) * per].reshape(
                npy, 2, ny, per
            )


def local_call(kernel, shape, name, *operands):
    vm = pl.BlockSpec(memory_space=pltpu.VMEM)
    return pl.pallas_call(
        kernel,
        out_shape=jax.ShapeDtypeStruct(shape, jnp.float32),
        in_specs=[vm] * len(operands),
        out_specs=vm,
        compiler_params=pltpu.CompilerParams(vmem_limit_bytes=40 * 2**20),
        name=name,
    )(*operands)


def projected_once(cotangent, sizes, npx, npy, others, beside_first, beside_second):
    NX, NY, NZ = sizes
    _, nx, ny, _ = cotangent.shape
    total = npx * npy
    nj = NZ // 2 // total
    cz, sz = waves(NZ, NZ // 2)
    cy, sy = waves(NY, NY)
    cx, sx = waves(NX, NX)
    shape = (total, 2, 3, ny, nj * nx)
    forward_z = np.stack([cz, -sz], 0).reshape(2, NZ, total, nj)
    forward_z = forward_z.transpose(3, 2, 0, 1).reshape(NZ, NZ)
    sent = local_call(
        functools.partial(forward_kernel, (total, nj, nx, ny)),
        shape,
        "forward",
        cotangent,
        halves(forward_z),
    )
    sent, others = lax.optimization_barrier((sent, others))
    got = lax.all_to_all(sent, ("px", "py"), 0, 0, tiled=True)
    first, halo_first = beside_first(*others)
    got, first = lax.optimization_barrier((got, first))
    forward_y = np.stack([np.stack([cy, -sy], 0), np.stack([sy, cy], 0)], 0)
    forward_y = forward_y.reshape(2, 2, npy, ny, NY).transpose(1, 4, 2, 0, 3)
    eye = np.eye(nj)
    forward_x = np.stack([cx, sx], 0).reshape(2, npx, nx, NX)
    forward_x = np.einsum("shxm,jk->hjxskm", forward_x, eye)
    backward_x = np.stack([cx, sx], 0).reshape(2, NX, npx, nx)
    backward_x = np.einsum("smhx,jk->jmshkx", backward_x, eye)
    backward_y = np.stack([np.stack([cy, sy], 0), np.stack([-sy, cy], 0)], 0)
    backward_y = backward_y.reshape(2, 2, NY, npy, ny).transpose(3, 1, 4, 0, 2)
    wide = nj * NX
    me = lax.axis_index("px") * npy + lax.axis_index("py")
    lane = jnp.arange(wide, dtype=jnp.int32)
    index_x, index_z = lane % NX, me * nj + lane // NX
    wave_x = jnp.where(index_x > NX // 2, index_x - NX, index_x).astype(jnp.float32)
    keep = ((index_x != NX // 2) & (index_z != NZ // 2)).astype(jnp.float32)
    lanes = jnp.stack([wave_x, index_z.astype(jnp.float32), keep])
    sent = local_call(
        functools.partial(middle_kernel, (npx, npy, ny, NY, wide)),
        shape,
        "middle",
        got,
        lanes,
        halves(forward_y.reshape(2 * NY, 2 * NY)),
        halves(forward_x.reshape(wide, 2 * wide)),
        halves(backward_x.reshape(wide, 2 * wide)),
        halves(backward_y.reshape(2 * NY, 2 * NY)),
    )
    sent, first, halo_first = lax.optimization_barrier((sent, first, halo_first))
    got = lax.all_to_all(sent, ("px", "py"), 0, 0, tiled=True)
    got, second = lax.optimization_barrier((got, beside_second(first, halo_first)))
    scale = mode_weights(NX, NY, NZ)
    backward_z = np.stack([(cz * scale).T, (-sz * scale).T], 0).reshape(2, total, nj, NZ)
    backward_z = backward_z.transpose(2, 1, 0, 3).reshape(NZ, NZ)
    lam = local_call(
        functools.partial(backward_kernel, (total, nj, nx, ny)),
        cotangent.shape,
        "backward",
        got,
        halves(backward_z),
    )
    return lam, second


def projected_twice(cotangent, sizes, npx, npy):
    NX, NY, NZ = sizes
    cz, sz = waves(NZ, NZ // 2)
    cy, sy = map(f32, waves(NY, NY))
    cx, sx = map(f32, waves(NX, NX))
    scale = mode_weights(NX, NY, NZ)
    stacked = jnp.stack(
        [einsum("cxyz,zk->cxyk", cotangent, f32(cz)), einsum("cxyz,zk->cxyk", cotangent, f32(-sz))]
    )
    re, im = lax.all_to_all(stacked, "py", split_axis=4, concat_axis=3, tiled=True)
    pair = jnp.stack(
        [
            einsum("cxyk,yl->ckxl", re, cy) + einsum("cxyk,yl->ckxl", im, sy),
            einsum("cxyk,yl->ckxl", im, cy) - einsum("cxyk,yl->ckxl", re, sy),
        ]
    )
    re, im = lax.all_to_all(pair, "px", split_axis=4, concat_axis=3, tiled=True)
    re, im = (
        einsum("ckxl,xm->cklm", re, cx) + einsum("ckxl,xm->cklm", im, sx),
        einsum("ckxl,xm->cklm", im, cx) - einsum("ckxl,xm->cklm", re, sx),
    )
    nk, nl = re.shape[1], re.shape[2]
    index_z = (lax.axis_index("py") * nk + jnp.arange(nk, dtype=jnp.int32))[:, None, None]
    index_y = (lax.axis_index("px") * nl + jnp.arange(nl, dtype=jnp.int32))[None, :, None]
    index_x = jnp.arange(NX, dtype=jnp.int32)[None, None, :]
    re, im = project(re, im, index_x, index_y, index_z, sizes)
    pair = jnp.stack(
        [
            einsum("cklm,mx->ckxl", re, cx) - einsum("cklm,mx->ckxl", im, sx),
            einsum("cklm,mx->ckxl", re, sx) + einsum("cklm,mx->ckxl", im, cx),
        ]
    )
    re, im = lax.all_to_all(pair, "px", split_axis=3, concat_axis=4, tiled=True)
    pair = jnp.stack(
        [
            einsum("ckxl,ly->cxyk", re, cy) - einsum("ckxl,ly->cxyk", im, sy),
            einsum("ckxl,ly->cxyk", re, sy) + einsum("ckxl,ly->cxyk", im, cy),
        ]
    )
    re, im = lax.all_to_all(pair, "py", split_axis=3, concat_axis=4, tiled=True)
    return einsum("cxyk,kz->cxyz", re, f32((cz * scale).T)) - einsum(
        "cxyk,kz->cxyz", im, f32((sz * scale).T)
    )


def body(velocity, cotangent, weight_in, bias_in, weight_out):
    npx, npy = lax.axis_size("px"), lax.axis_size("py")
    _, nx, ny, NZ = velocity.shape
    sizes = (nx * npx, ny * npy, NZ)
    spacings = tuple(2.0 * math.pi / size for size in sizes)
    rows = rows_of(ny)

    def beside_first(velocity, weight_in, bias_in, weight_out):
        w1, bias = input_weights(weight_in, bias_in, ny, rows)
        w2, w3 = output_weights(weight_in, weight_out, ny, rows)
        return (w1, bias, w2, w3), (velocity,) + halo(velocity, "py", 2, 3)

    def beside_second(first, halo_first):
        w1, bias, w2, w3 = first
        wide = widened(*halo_first)
        low, up = halo(wide, "px", 1, 3)
        vel_ext = joined(low, wide, up)
        slope, grads = velocity_step(vel_ext, w1, bias, nx, ny, spacings)
        return vel_ext, slope, grads, w2, w3

    others = (velocity, weight_in, bias_in, weight_out)
    if (NZ // 2) % (npx * npy) == 0 and nx * (NZ // 2) % (npx * npy * LANES) == 0 and ny % 8 == 0:
        lam, second = projected_once(cotangent, sizes, npx, npy, others, beside_first, beside_second)
    else:
        lam = projected_twice(cotangent, sizes, npx, npy)
        second = beside_second(*beside_first(*others))
    vel_ext, slope, grads, w2, w3 = second
    return closure_step(vel_ext, bordered(lam), slope, grads, w2, w3, nx, ny, spacings)


def solution(mesh):
    placed = (P(None, "px", "py", None), P(None, "px", "py", None), P(), P(), P())
    return jax.shard_map(
        body, mesh=mesh, in_specs=placed, out_specs=P(None, "px", "py", None), check_vma=False
    )
```
